512 devices in a mesh: rows: 64 (over z, y_hi, core), cols: 8 (over y_lo, x).
Axes of the slice: x: 4, y: 8 (y_hi: 4, y_lo: 2; y = y_hi * 2 + y_lo), z: 8, core: 2. Of those that a mesh axis runs over, the one named last changes fastest.
Arguments:
- momentum: bfloat16 [25600, 2816], P('rows', 'cols'), may hold values from -6 to 6
Outputs:
- iterate: bfloat16 [25600, 2816], P('rows', 'cols')
The draws below stay inside these ranges and needn't reach their ends.
All inputs are finite; a program needn't handle non-finite values.
Results may differ from the reference program's by a relative error of at most 0.01.
Values may be sent and summed in bfloat16 or wider, within the bound.
A program may use at most 64 MiB of HBM per device.

```python
import jax
import jax.numpy as jnp
from jax import lax

ROWS = 25600
COLS = 2816


def steps_of(rng, shape, split, smallest, top_value):
    def one(dim, parts):
        draws = jax.random.uniform(jax.random.fold_in(jax.random.fold_in(rng, 6), dim), (parts,), jnp.float32, smallest / len(split), top_value / len(split))
        return jnp.repeat(jnp.exp(draws), shape[dim] // parts).reshape((-1,) + (1,) * (len(shape) - dim - 1))

    gain = one(*split[0])
    for cut in split[1:]:
        gain = gain * one(*cut)
    return gain


def centred(rng, shape, scale, bound, shards=(), kind=jnp.bfloat16):
    level = steps_of(rng, shape, shards, -0.22, 0.18) if shards else 1.0
    values = jax.random.normal(rng, shape, jnp.float32) * scale * level
    return jnp.minimum(jnp.maximum(values, -bound), bound).astype(kind)


def setup_inputs(seed: int = 0) -> dict:
    seeds = jax.random.split(jax.random.key(seed), 2)
    return {
        "momentum": centred(seeds[0], (ROWS, COLS), 1.0, 6.0, ((0, 64), (1, 8))),
    }


coef_a = 3.4445
coef_b = -4.7750
coef_c = 2.0315


def reference(momentum):
    gram_full = lax.dot_general(momentum, momentum, (((0,), (0,)), ((), ())), preferred_element_type=jnp.float32)
    gram = (gram_full / ROWS).astype(jnp.bfloat16)
    square = jnp.dot(gram, gram, preferred_element_type=jnp.float32)
    poly = (coef_b * gram.astype(jnp.float32) + coef_c * square).astype(jnp.bfloat16)
    update = jnp.dot(momentum, poly, preferred_element_type=jnp.float32)
    return (coef_a * momentum.astype(jnp.float32) + update).astype(jnp.bfloat16)
```

```python
import jax
import jax.numpy as jnp
from jax import lax
from jax.experimental import pallas as pl
from jax.experimental.pallas import tpu as pltpu
from jax.sharding import PartitionSpec as P

ROWS = 25600

coef_a = 3.4445
coef_b = -4.775
coef_c = 2.0315

NZ, NY, NX = 8, 4, 4
NB = 8
MESH = pl.DeviceIdType.MESH
F32, BF16 = jnp.float32, jnp.bfloat16


def kernel(
    x_hbm, o_ref, xx, sb, rb, yb, gl, gr, pf, lt,
    loc, xs, xr, cs, cr, zs, zr, ys, yr, gzs, gzr, gxs, gxr, gcs, gcr, pzs, pzr, pcs, pcr,
):
    m, w = x_hbm.shape
    h = w // 2
    r, c = lax.axis_index("rows"), lax.axis_index("cols")
    z, yh, k = r // (NY * 2), lax.rem(r // 2, NY), lax.rem(r, 2)
    yl, x = c // NX, lax.rem(c, NX)

    def rid(z=z, yh=yh, k=k):
        return (z * NY + yh) * 2 + k

    def cid(yl=yl, x=x):
        return yl * NX + x

    def at_x(d):
        return lax.rem(x + d, NX)

    def at_z(d):
        return lax.rem(z + d, NZ)

    def at_y(d):
        return lax.rem(yh + d, NY)

    sends = []

    def send(src, dst, ss, rs, to):
        copy = pltpu.make_async_remote_copy(
            src_ref=src, dst_ref=dst, send_sem=ss, recv_sem=rs, device_id=to, device_id_type=MESH
        )
        copy.start()
        sends.append(copy)

    def arrived(dst, ss, rs):
        pltpu.make_async_remote_copy(
            src_ref=dst, dst_ref=dst, send_sem=ss, recv_sem=rs, device_id=core, device_id_type=MESH
        ).wait_recv()

    core = (rid(k=1 - k), c)
    ypair = (r, cid(yl=1 - yl))
    xdev = [(r, cid(x=at_x(d))) for d in range(NX)]
    zdev = [(rid(z=at_z(d)), c) for d in range(NZ)]
    ydev = [(rid(yh=at_y(d)), c) for d in range(NY)]

    mine = xx.at[c, pl.ds(k * m, m)]
    own = pltpu.make_async_copy(x_hbm, mine, loc)
    own.start()

    barrier = pltpu.get_barrier_semaphore()
    partners = [core, ypair] + xdev[1:] + zdev[1:] + ydev[1:]
    for to in partners:
        pl.semaphore_signal(barrier, inc=1, device_id=to, device_id_type=MESH)
    pl.semaphore_wait(barrier, len(partners))
    own.wait()

    def half(b):
        return xx.at[b, pl.ds(k * m, m)]

    def other(b):
        return xx.at[b, pl.ds((1 - k) * m, m)]

    send(mine, mine, xs.at[0], xr.at[c], ypair)
    for i, d in enumerate((1, 3, 2)):
        send(mine, mine, xs.at[1 + i], xr.at[c], xdev[d])
    send(mine, mine, cs.at[0], cr.at[c], core)

    c2 = cid(yl=1 - yl)
    order = [c, c2] + [cid(x=at_x(d)) for d in (1, 3, 2)] + [cid(yl=1 - yl, x=at_x(d)) for d in (1, 3, 2)]
    pick = (
        lax.broadcasted_iota(jnp.int32, (h, w), 1) == lax.broadcasted_iota(jnp.int32, (h, w), 0) + k * h
    ).astype(BF16)
    for i, b in enumerate(order):
        if i > 0:
            arrived(half(b), xs.at[0], xr.at[b])
            if i == 1:
                for j, d in enumerate((1, 3, 2)):
                    send(half(b), half(b), xs.at[4 + j], xr.at[b], xdev[d])
            send(half(b), half(b), cs.at[i], cr.at[b], core)
        arrived(other(b), xs.at[0], cr.at[b])
        if i == 0:
            lt[...] = lax.dot_general(
                pick, xx[c], (((1,), (1,)), ((), ())), preferred_element_type=F32
            ).astype(BF16)
        sb[i] = jnp.dot(lt[...], xx[b], preferred_element_type=F32).astype(BF16)

        @pl.when(b != z)
        def _():
            pltpu.make_async_remote_copy(
                src_ref=sb.at[i], dst_ref=rb.at[z], send_sem=zs.at[i], recv_sem=zr.at[z],
                device_id=(rid(z=b), c), device_id_type=MESH,
            ).start()

        @pl.when(b == z)
        def _():
            rb[z] = sb[i]

    for d in range(1, NZ):
        s = at_z(d)
        arrived(rb.at[s], zs.at[0], zr.at[s])
    part = rb[0].astype(F32)
    for s in range(1, NZ):
        part = part + rb[s].astype(F32)
    yb[yh] = part.astype(BF16)
    for d in (1, 3, 2):
        send(yb.at[yh], yb.at[yh], ys.at[d], yr.at[yh], ydev[d])
    for d in (1, 3, 2):
        s = at_y(d)
        arrived(yb.at[s], ys.at[0], yr.at[s])
    total = yb[0].astype(F32)
    for s in range(1, NY):
        total = total + yb[s].astype(F32)
    gram = (total / ROWS).astype(BF16)
    top = pl.ds(k * h, h)
    low = pl.ds((1 - k) * h, h)
    gl[z] = gram
    gr[c, top, :] = gram

    g0 = gr.at[c, top]
    send(gl.at[z], gl.at[z], gzs.at[0], gzr.at[z], zdev[1])
    send(gl.at[z], gl.at[z], gzs.at[4], gzr.at[z], zdev[7])
    send(g0, g0, gxs.at[0], gxr.at[c], ypair)
    for i, d in enumerate((1, 3, 2)):
        send(g0, g0, gxs.at[1 + i], gxr.at[c], xdev[d])
    send(g0, g0, gcs.at[0], gcr.at[c], core)

    def ring(buf, ss, rs, step):
        right, left = at_z(NZ - 1 - step), at_z(1 + step)
        arrived(buf(right), ss.at[0], rs.at[right])
        if step < 3:
            send(buf(right), buf(right), ss.at[1 + step], rs.at[right], zdev[1])
        if step < 3:
            arrived(buf(left), ss.at[0], rs.at[left])
            if step < 2:
                send(buf(left), buf(left), ss.at[5 + step], rs.at[left], zdev[7])
            return [right, left]
        return [right]

    def column(i):
        b = order[i]
        g = gr.at[b, top]
        arrived(g, gxs.at[0], gxr.at[b])
        if i == 1:
            for j, d in enumerate((1, 3, 2)):
                send(g, g, gxs.at[4 + j], gxr.at[b], xdev[d])
        send(g, g, gcs.at[i], gcr.at[b], core)

    column(1)
    for step in range(4):
        ring(lambda s: gl.at[s], gzs, gzr, step)
        if step < 3:
            column(2 + 2 * step)
            column(3 + 2 * step)
    for b in order:
        g = gr.at[b, low]
        arrived(g, gcs.at[0], gcr.at[b])
    square = jnp.dot(gl[0], gr[0], preferred_element_type=F32)
    for s in range(1, NB):
        square = square + jnp.dot(gl[s], gr[s], preferred_element_type=F32)
    pf[z, top, :] = (coef_b * gram.astype(F32) + coef_c * square).astype(BF16)

    def poly(s):
        return pf.at[s, top]

    send(poly(z), poly(z), pzs.at[0], pzr.at[z], zdev[1])
    send(poly(z), poly(z), pzs.at[4], pzr.at[z], zdev[7])
    send(poly(z), poly(z), pcs.at[0], pcr.at[z], core)

    def term(s):
        arrived(pf.at[s, low], pcs.at[0], pcr.at[s])
        return lax.dot_general(
            xx[s, pl.ds(k * m, m)], pf[s], (((1,), (1,)), ((), ())), preferred_element_type=F32
        )

    update = term(z)
    n = 1
    for step in range(4):
        got = ring(poly, pzs, pzr, step)
        for s in got:
            send(poly(s), poly(s), pcs.at[n], pcr.at[s], core)
            n += 1
        for s in got:
            update = update + term(s)
    o_ref[...] = (coef_a * xx[c, pl.ds(k * m, m)].astype(F32) + update).astype(BF16)

    for copy in sends:
        copy.wait_send()
    for i, b in enumerate(order):

        @pl.when(b != z)
        def _():
            pltpu.make_async_remote_copy(
                src_ref=sb.at[i], dst_ref=rb.at[z], send_sem=zs.at[i], recv_sem=zr.at[z],
                device_id=core, device_id_type=MESH,
            ).wait_send()


def local(momentum):
    m, w = momentum.shape
    h = w // 2
    dma = lambda n: pltpu.SemaphoreType.DMA((n,))
    return pl.pallas_call(
        kernel,
        out_shape=jax.ShapeDtypeStruct((m, w), BF16),
        in_specs=[pl.BlockSpec(memory_space=pl.ANY)],
        out_specs=pl.BlockSpec(memory_space=pltpu.VMEM),
        scratch_shapes=[
            pltpu.VMEM((NB, 2 * m, w), BF16),
            pltpu.VMEM((NB, h, w), BF16),
            pltpu.VMEM((NZ, h, w), BF16),
            pltpu.VMEM((NY, h, w), BF16),
            pltpu.VMEM((NZ, h, w), BF16),
            pltpu.VMEM((NB, w, w), BF16),
            pltpu.VMEM((NZ, w, w), BF16),
            pltpu.VMEM((h, 2 * m), BF16),
            pltpu.SemaphoreType.DMA,
            dma(7), dma(8), dma(8), dma(8),
            dma(8), dma(8), dma(4), dma(4),
            dma(7), dma(8), dma(7), dma(8), dma(8), dma(8),
            dma(7), dma(8), dma(8), dma(8),
        ],
        compiler_params=pltpu.CompilerParams(
            collective_id=0, has_side_effects=True, vmem_limit_bytes=48 << 20
        ),
        name="newton_schulz",
    )(momentum)


def solution(mesh):
    return jax.shard_map(
        local,
        mesh=mesh,
        in_specs=(P("rows", "cols"),),
        out_specs=P("rows", "cols"),
        check_vma=False,
    )
```

```python
import jax
import jax.numpy as jnp
from jax import lax
from jax.experimental import pallas as pl
from jax.experimental.pallas import tpu as pltpu
from jax.sharding import PartitionSpec as P

ROWS = 25600

coef_a = 3.4445
coef_b = -4.775
coef_c = 2.0315

NZ, NY, NX = 8, 4, 4
NB = 8
MESH = pl.DeviceIdType.MESH
F32, BF16 = jnp.float32, jnp.bfloat16


def kernel(
    x_hbm, o_ref, xx, sb, rb, yb, gl, gr, pf, lt,
    loc, xs, xr, cs, cr, zs, zr, ys, yr, gzs, gzr, gys, gyr, gxs, gxs2, gxr, gcs, gcr, pzs, pzr, pcs, pcr,
):
    m, w = x_hbm.shape
    h = w // 2
    cut = -(-h // 32) * 16
    r, c = lax.axis_index("rows"), lax.axis_index("cols")
    z, yh, k = r // (NY * 2), lax.rem(r // 2, NY), lax.rem(r, 2)
    yl, x = c // NX, lax.rem(c, NX)

    def rid(z=z, yh=yh, k=k):
        return (z * NY + yh) * 2 + k

    def cid(yl=yl, x=x):
        return yl * NX + x

    def at_x(d):
        return lax.rem(x + d, NX)

    def at_z(d):
        return lax.rem(z + d, NZ)

    def at_y(d):
        return lax.rem(yh + d, NY)

    sends = []

    def send(src, dst, ss, rs, to):
        copy = pltpu.make_async_remote_copy(
            src_ref=src, dst_ref=dst, send_sem=ss, recv_sem=rs, device_id=to, device_id_type=MESH
        )
        copy.start()
        sends.append(copy)

    def arrived(dst, ss, rs):
        pltpu.make_async_remote_copy(
            src_ref=dst, dst_ref=dst, send_sem=ss, recv_sem=rs, device_id=core, device_id_type=MESH
        ).wait_recv()

    core = (rid(k=1 - k), c)
    ypair = (r, cid(yl=1 - yl))
    xdev = [(r, cid(x=at_x(d))) for d in range(NX)]
    zdev = [(rid(z=at_z(d)), c) for d in range(NZ)]
    ydev = [(rid(yh=at_y(d)), c) for d in range(NY)]

    mine = xx.at[c, pl.ds(k * m, m)]
    own = pltpu.make_async_copy(x_hbm, mine, loc)
    own.start()

    barrier = pltpu.get_barrier_semaphore()
    partners = [core, ypair] + xdev[1:] + zdev[1:] + ydev[1:]
    for to in partners:
        pl.semaphore_signal(barrier, inc=1, device_id=to, device_id_type=MESH)
    pl.semaphore_wait(barrier, len(partners))
    own.wait()

    def half(b):
        return xx.at[b, pl.ds(k * m, m)]

    def other(b):
        return xx.at[b, pl.ds((1 - k) * m, m)]

    send(mine, mine, xs.at[0], xr.at[c], ypair)
    for i, d in enumerate((1, 3, 2)):
        send(mine, mine, xs.at[1 + i], xr.at[c], xdev[d])
    send(mine, mine, cs.at[0], cr.at[c], core)

    c2 = cid(yl=1 - yl)
    order = [c, c2] + [cid(x=at_x(d)) for d in (1, 3, 2)] + [cid(yl=1 - yl, x=at_x(d)) for d in (1, 3, 2)]
    pick = (
        lax.broadcasted_iota(jnp.int32, (h, w), 1) == lax.broadcasted_iota(jnp.int32, (h, w), 0) + k * h
    ).astype(BF16)
    for i, b in enumerate(order):
        if i > 0:
            arrived(half(b), xs.at[0], xr.at[b])
            if i == 1:
                for j, d in enumerate((1, 3, 2)):
                    send(half(b), half(b), xs.at[4 + j], xr.at[b], xdev[d])
            send(half(b), half(b), cs.at[i], cr.at[b], core)
        arrived(other(b), xs.at[0], cr.at[b])
        if i == 0:
            lt[...] = lax.dot_general(
                pick, xx[c], (((1,), (1,)), ((), ())), preferred_element_type=F32
            ).astype(BF16)
        sb[i] = jnp.dot(lt[...], xx[b], preferred_element_type=F32).astype(BF16)

        @pl.when(b != z)
        def _():
            pltpu.make_async_remote_copy(
                src_ref=sb.at[i], dst_ref=rb.at[z], send_sem=zs.at[i], recv_sem=zr.at[z],
                device_id=(rid(z=b), c), device_id_type=MESH,
            ).start()

        @pl.when(b == z)
        def _():
            rb[z] = sb[i]

    for d in range(1, NZ):
        s = at_z(d)
        arrived(rb.at[s], zs.at[0], zr.at[s])
    part = rb[0].astype(F32)
    for s in range(1, NZ):
        part = part + rb[s].astype(F32)
    yb[yh] = part.astype(BF16)
    for d in (1, 3, 2):
        send(yb.at[yh], yb.at[yh], ys.at[d], yr.at[yh], ydev[d])
    for d in (1, 3, 2):
        s = at_y(d)
        arrived(yb.at[s], ys.at[0], yr.at[s])
    total = yb[0].astype(F32)
    for s in range(1, NY):
        total = total + yb[s].astype(F32)
    gram = (total / ROWS).astype(BF16)
    top = pl.ds(k * h, h)
    low = pl.ds((1 - k) * h, h)
    gl[z] = gram
    gr[c, top, :] = gram

    g0 = gr.at[c, top]
    def part_of(n):
        return pl.ds(0, cut) if n == 0 else pl.ds(cut, h - cut)

    def g_row(s, n):
        return gl.at[s, part_of(n)]

    def g_col(b, n):
        return gr.at[b, pl.ds(k * h + n * cut, h - cut if n else cut)]

    def p_row(s, n):
        return pf.at[s, pl.ds(k * h + n * cut, h - cut if n else cut)]

    def ring_hop(buf, ss, rs, dev, slots, hop, right, n):
        reach = len(slots) // 2 - (right == n)
        if hop > reach:
            return
        s = slots[-hop if right else hop] if hop else slots[0]
        if hop:
            arrived(buf(s, n), ss.at[0, 0, 0], rs.at[s, n])
        if hop < reach:
            send(buf(s, n), buf(s, n), ss.at[hop, right, n], rs.at[s, n], dev[1 if right else -1])

    def ring_step(*args):
        for right, n in ((1, 0), (0, 1), (1, 1), (0, 0)):
            ring_hop(*args, right, n)

    zslots = [at_z(d) for d in range(NZ)]
    xslots = [cid(x=at_x(d)) for d in range(NX)]
    xslots2 = [cid(yl=1 - yl, x=at_x(d)) for d in range(NX)]
    zring = (g_row, gzs, gzr, zdev, zslots)
    xring = (g_col, gxs, gxr, xdev, xslots)
    xring2 = (g_col, gxs2, gxr, xdev, xslots2)

    for n in range(2):
        send(g_col(c, n), g_col(c, n), gys.at[n], gyr.at[n], ypair)
    ring_step(*xring, 0)
    ring_step(*zring, 0)
    send(gr.at[c, top], gr.at[c, top], gcs.at[0], gcr.at[c], core)

    def hand_on(slots, first, ds):
        for i, d in enumerate(ds):
            g = gr.at[slots[d], top]
            send(g, g, gcs.at[first + i], gcr.at[slots[d]], core)

    for n in range(2):
        arrived(g_col(c2, n), gys.at[0], gyr.at[n])
    ring_step(*xring2, 0)
    hand_on(xslots2, 1, (0,))
    ring_step(*xring, 1)
    ring_step(*zring, 1)
    hand_on(xslots, 2, (1, 3))
    ring_step(*xring, 2)
    ring_step(*zring, 2)
    hand_on(xslots, 4, (2,))
    ring_step(*xring2, 1)
    hand_on(xslots2, 5, (1, 3))
    ring_step(*zring, 3)
    ring_step(*xring2, 2)
    hand_on(xslots2, 7, (2,))
    ring_step(*zring, 4)
    for b in order:
        g = gr.at[b, low]
        arrived(g, gcs.at[0], gcr.at[b])
    square = jnp.dot(gl[0], gr[0], preferred_element_type=F32)
    for s in range(1, NB):
        square = square + jnp.dot(gl[s], gr[s], preferred_element_type=F32)
    pf[z, top, :] = (coef_b * gram.astype(F32) + coef_c * square).astype(BF16)
    pring = (p_row, pzs, pzr, zdev, zslots)
    ring_step(*pring, 0)
    send(pf.at[z, top], pf.at[z, top], pcs.at[0], pcr.at[z], core)

    def term(s):
        arrived(pf.at[s, low], pcs.at[0], pcr.at[s])
        return lax.dot_general(
            xx[s, pl.ds(k * m, m)], pf[s], (((1,), (1,)), ((), ())), preferred_element_type=F32
        )

    update = term(z)
    n = 1
    for step in range(1, 5):
        ring_step(*pring, step)
        got = [zslots[-step], zslots[step]] if step < 4 else [zslots[4]]
        for s in got:
            send(pf.at[s, top], pf.at[s, top], pcs.at[n], pcr.at[s], core)
            n += 1
        for s in got:
            update = update + term(s)
    o_ref[...] = (coef_a * xx[c, pl.ds(k * m, m)].astype(F32) + update).astype(BF16)
    for copy in sends:
        copy.wait_send()
    for i, b in enumerate(order):

        @pl.when(b != z)
        def _():
            pltpu.make_async_remote_copy(
                src_ref=sb.at[i], dst_ref=rb.at[z], send_sem=zs.at[i], recv_sem=zr.at[z],
                device_id=core, device_id_type=MESH,
            ).wait_send()


def local(momentum):
    m, w = momentum.shape
    h = w // 2
    dma = lambda *n: pltpu.SemaphoreType.DMA(n)
    return pl.pallas_call(
        kernel,
        out_shape=jax.ShapeDtypeStruct((m, w), BF16),
        in_specs=[pl.BlockSpec(memory_space=pl.ANY)],
        out_specs=pl.BlockSpec(memory_space=pltpu.VMEM),
        scratch_shapes=[
            pltpu.VMEM((NB, 2 * m, w), BF16),
            pltpu.VMEM((NB, h, w), BF16),
            pltpu.VMEM((NZ, h, w), BF16),
            pltpu.VMEM((NY, h, w), BF16),
            pltpu.VMEM((NZ, h, w), BF16),
            pltpu.VMEM((NB, w, w), BF16),
            pltpu.VMEM((NZ, w, w), BF16),
            pltpu.VMEM((h, 2 * m), BF16),
            pltpu.SemaphoreType.DMA,
            dma(7), dma(8), dma(8), dma(8),
            dma(8), dma(8), dma(4), dma(4),
            dma(4, 2, 2), dma(8, 2), dma(2), dma(2), dma(2, 2, 2), dma(2, 2, 2), dma(8, 2), dma(8), dma(8),
            dma(4, 2, 2), dma(8, 2), dma(8), dma(8),
        ],
        compiler_params=pltpu.CompilerParams(
            collective_id=0, has_side_effects=True, vmem_limit_bytes=48 << 20
        ),
        name="newton_schulz",
    )(momentum)


def solution(mesh):
    return jax.shard_map(
        local,
        mesh=mesh,
        in_specs=(P("rows", "cols"),),
        out_specs=P("rows", "cols"),
        check_vma=False,
    )
```

```python
import jax
import jax.numpy as jnp
from jax import lax
from jax.experimental import pallas as pl
from jax.experimental.pallas import tpu as pltpu
from jax.sharding import PartitionSpec as P

ROWS = 25600

coef_a = 3.4445
coef_b = -4.775
coef_c = 2.0315

NZ, NY, NX = 8, 4, 4
NB = 8
EARLY = 4
MESH = pl.DeviceIdType.MESH
F32, BF16 = jnp.float32, jnp.bfloat16


def kernel(
    x_hbm, o_ref, xx, sb, rb, eb, yb, qb, zb, tot, gl, gr, pf, lt,
    loc, ws, wr, xs, xr, xs2, xr2, vys, vyr, cs, cr, zs, zr, zqr, ys, yr, as_, ar, gzs, gzr, gys, gyr, gxs, gxs2, gxr, gcs, gcr, pzs, pzr, pcs, pcr,
):
    m, w = x_hbm.shape
    h = w // 2
    q = qb.shape[1]
    hp = NY * q
    cut = -(-h // 32) * 16
    mid = -(-m // 32) * 16
    qtr = -(-mid // 32) * 16
    r, c = lax.axis_index("rows"), lax.axis_index("cols")
    z, yh, k = r // (NY * 2), lax.rem(r // 2, NY), lax.rem(r, 2)
    yl, x = c // NX, lax.rem(c, NX)

    def rid(z=z, yh=yh, k=k):
        return (z * NY + yh) * 2 + k

    def cid(yl=yl, x=x):
        return yl * NX + x

    def at_x(d):
        return lax.rem(x + d, NX)

    def at_z(d):
        return lax.rem(z + d, NZ)

    def at_y(d):
        return lax.rem(yh + d, NY)

    sends = []

    def send(src, dst, ss, rs, to):
        copy = pltpu.make_async_remote_copy(
            src_ref=src, dst_ref=dst, send_sem=ss, recv_sem=rs, device_id=to, device_id_type=MESH
        )
        copy.start()
        sends.append(copy)

    def arrived(dst, ss, rs):
        pltpu.make_async_remote_copy(
            src_ref=dst, dst_ref=dst, send_sem=ss, recv_sem=rs, device_id=core, device_id_type=MESH
        ).wait_recv()

    core = (rid(k=1 - k), c)
    ypair = (r, cid(yl=1 - yl))
    xdev = [(r, cid(x=at_x(d))) for d in range(NX)]
    zdev = [(rid(z=at_z(d)), c) for d in range(NZ)]
    ydev = [(rid(yh=at_y(d)), c) for d in range(NY)]

    mine = xx.at[c, pl.ds(k * m, m)]
    own = pltpu.make_async_copy(x_hbm, mine, loc)
    own.start()

    barrier = pltpu.get_barrier_semaphore()
    partners = [core, ypair] + xdev[1:] + zdev[1:] + ydev[1:]
    for to in partners:
        pl.semaphore_signal(barrier, inc=1, device_id=to, device_id_type=MESH)
    pl.semaphore_wait(barrier, len(partners))
    own.wait()

    def half(b):
        return xx.at[b, pl.ds(k * m, m)]

    def other(b):
        return xx.at[b, pl.ds((1 - k) * m, m)]

    c2 = cid(yl=1 - yl)
    order = [c, c2] + [cid(x=at_x(d)) for d in (1, 3, 2)] + [cid(yl=1 - yl, x=at_x(d)) for d in (1, 3, 2)]

    def owner(b):
        return lax.rem(b, NX) * 2 + b // NX

    def block(s):
        return s % 2 * NX + s // 2 if isinstance(s, int) else lax.rem(s, 2) * NX + s // 2

    def part_of(n):
        return pl.ds(0, cut) if n == 0 else pl.ds(cut, h - cut)

    def g_row(s, n):
        return gl.at[s, part_of(n)]

    def g_col(b, n):
        return gr.at[b, pl.ds(k * h + n * cut, h - cut if n else cut)]

    def p_row(s, n):
        return pf.at[s, pl.ds(k * h + n * cut, h - cut if n else cut)]

    def ring_hop(buf, ss, rs, dev, slots, hop, right, n):
        reach = len(slots) // 2 - (right == n)
        if hop > reach:
            return
        s = slots[-hop if right else hop] if hop else slots[0]
        if hop:
            arrived(buf(s, n), ss.at[0, 0, 0], rs.at[s, n])
        if hop < reach:
            send(buf(s, n), buf(s, n), ss.at[hop, right, n], rs.at[s, n], dev[1 if right else -1])

    def ring_step(*args):
        for right, n in ((1, 0), (0, 1), (1, 1), (0, 0)):
            ring_hop(*args, right, n)

    zslots = [at_z(d) for d in range(NZ)]
    xslots = [cid(x=at_x(d)) for d in range(NX)]
    xslots2 = [cid(yl=1 - yl, x=at_x(d)) for d in range(NX)]
    zring = (g_row, gzs, gzr, zdev, zslots)
    xring = (g_col, gxs, gxr, xdev, xslots)
    xring2 = (g_col, gxs2, gxr, xdev, xslots2)

    def x_half(b, n):
        return xx.at[b, pl.ds(k * m + n * mid, m - mid if n else mid)]

    def x_quarter(b, n):
        return xx.at[b, pl.ds(k * m + n * qtr, mid - qtr if n else qtr)]

    def hand(i):
        send(half(order[i]), half(order[i]), cs.at[i], cr.at[order[i]], core)

    def partial(i):
        b = order[i]
        if i:
            arrived(other(b), cs.at[0], cr.at[b])
        sb[i] = jnp.dot(lt[...], xx[b], preferred_element_type=F32).astype(BF16)
        if i < EARLY:
            to_owner(i, sb.at[i], rb, zr)
        else:
            j = i - EARLY
            yb[j, yh] = sb[i, quarter(yh)]
            for d in (1, 3, 2):
                send(sb.at[i, quarter(at_y(d))], yb.at[j, yh], ys.at[j, d], yr.at[j, yh], ydev[d])

    def quarter(p):
        return pl.ds(pl.multiple_of(p * q, q), q)

    def to_owner(i, src, dst, rs):
        to = owner(order[i])

        @pl.when(to != z)
        def _():
            pltpu.make_async_remote_copy(
                src_ref=src, dst_ref=dst.at[z], send_sem=zs.at[i], recv_sem=rs.at[z],
                device_id=(rid(z=to), c), device_id_type=MESH,
            ).start()

        @pl.when(to == z)
        def _():
            dst[z] = src[...]

    def late(i):
        j = i - EARLY
        add_up(yb.at[j], lambda s: yr.at[j, s], [at_y(d) for d in (1, 3, 2)], qb.at[j])
        to_owner(i, qb.at[j], zb, zqr)

    def add_up(buf, rs, others, out):
        for s in others:
            arrived(buf.at[s], zs.at[0], rs(s))
        value = buf[0].astype(F32)
        for s in range(1, buf.shape[0]):
            value = value + buf[s].astype(F32)
        out[...] = value.astype(out.dtype)

    def over(i, d):
        v = x_half(order[i], 1)
        send(v, v, vys.at[d - 1], vyr.at[order[i]], ypair)

    def back(i):
        arrived(x_half(order[i], 1), vys.at[0], vyr.at[order[i]])

    rring = (x_half, xs, xr, xdev, xslots)
    rring2 = (x_quarter, xs2, xr2, xdev, xslots2)
    for n in range(2):
        send(x_half(c, n), x_half(c, n), ws.at[n], wr.at[n], ypair)
    ring_step(*rring, 0)
    hand(0)
    pick = (
        lax.broadcasted_iota(jnp.int32, (hp, w), 1) == lax.broadcasted_iota(jnp.int32, (hp, w), 0) + k * h
    ).astype(BF16)
    arrived(other(c), cs.at[0], cr.at[c])
    lt[...] = lax.dot_general(
        pick, xx[c], (((1,), (1,)), ((), ())), preferred_element_type=F32
    ).astype(BF16)
    partial(0)
    for n in range(2):
        arrived(x_half(c2, n), ws.at[0], wr.at[n])
    hand(1)
    ring_step(*rring, 1)
    over(2, 1)
    over(3, 3)
    hand(2)
    hand(3)
    ring_step(*rring2, 0)
    partial(1)
    partial(2)
    partial(3)
    ring_step(*rring, 2)
    over(4, 2)
    hand(4)
    partial(4)
    ring_step(*rring2, 1)
    for i in (5, 6):
        back(i)
        hand(i)
    partial(5)
    partial(6)
    late(4)
    ring_step(*rring2, 2)
    back(7)
    hand(7)
    late(5)
    late(6)
    partial(7)
    late(7)

    mine_early = owner(order[0]) == z
    for i in range(1, EARLY):
        mine_early = jnp.logical_or(mine_early, owner(order[i]) == z)
    zothers = [at_z(d) for d in range(1, NZ)]

    @pl.when(mine_early)
    def _():
        add_up(rb, lambda s: zr.at[s], zothers, eb)
        yb[NB - EARLY, yh] = eb[quarter(yh)]
        for d in (1, 3, 2):
            pltpu.make_async_remote_copy(
                src_ref=eb.at[quarter(at_y(d))], dst_ref=yb.at[NB - EARLY, yh], send_sem=ys.at[NB - EARLY, d],
                recv_sem=yr.at[NB - EARLY, yh], device_id=ydev[d], device_id_type=MESH,
            ).start()
        add_up(yb.at[NB - EARLY], lambda s: yr.at[NB - EARLY, s], [at_y(d) for d in (1, 3, 2)], tot)

    @pl.when(jnp.logical_not(mine_early))
    def _():
        add_up(zb, lambda s: zqr.at[s], zothers, tot)

    gl[z, quarter(yh)] = (tot[...] / ROWS).astype(BF16)
    for d in (1, 3, 2):
        g = gl.at[z, quarter(yh)]
        send(g, g, as_.at[d], ar.at[yh], ydev[d])
    for d in (1, 3, 2):
        arrived(gl.at[z, quarter(at_y(d))], as_.at[0], ar.at[at_y(d)])
    top = pl.ds(k * h, h)
    low = pl.ds((1 - k) * h, h)
    gram = gl[z, pl.ds(0, h)]
    gr[c, top, :] = gram

    for n in range(2):
        send(g_col(c, n), g_col(c, n), gys.at[n], gyr.at[n], ypair)
    ring_step(*xring, 0)
    ring_step(*zring, 0)
    send(gr.at[c, top], gr.at[c, top], gcs.at[0], gcr.at[c], core)

    def hand_on(slots, first, ds):
        for i, d in enumerate(ds):
            g = gr.at[slots[d], top]
            send(g, g, gcs.at[first + i], gcr.at[slots[d]], core)

    for n in range(2):
        arrived(g_col(c2, n), gys.at[0], gyr.at[n])
    ring_step(*xring2, 0)
    hand_on(xslots2, 1, (0,))
    ring_step(*xring, 1)
    ring_step(*zring, 1)
    hand_on(xslots, 2, (1, 3))
    ring_step(*xring, 2)
    ring_step(*zring, 2)
    hand_on(xslots, 4, (2,))
    ring_step(*xring2, 1)
    hand_on(xslots2, 5, (1, 3))
    ring_step(*zring, 3)
    ring_step(*xring2, 2)
    hand_on(xslots2, 7, (2,))
    ring_step(*zring, 4)
    for b in order:
        g = gr.at[b, low]
        arrived(g, gcs.at[0], gcr.at[b])
    square = jnp.dot(gl[0, :h], gr[block(0)], preferred_element_type=F32)
    for s in range(1, NB):
        square = square + jnp.dot(gl[s, :h], gr[block(s)], preferred_element_type=F32)
    pf[z, top, :] = (coef_b * gram.astype(F32) + coef_c * square).astype(BF16)
    pring = (p_row, pzs, pzr, zdev, zslots)
    ring_step(*pring, 0)
    send(pf.at[z, top], pf.at[z, top], pcs.at[0], pcr.at[z], core)

    def term(s):
        arrived(pf.at[s, low], pcs.at[0], pcr.at[s])
        return lax.dot_general(
            xx[block(s), pl.ds(k * m, m)], pf[s], (((1,), (1,)), ((), ())), preferred_element_type=F32
        )

    update = term(z)
    n = 1
    for step in range(1, 5):
        ring_step(*pring, step)
        got = [zslots[-step], zslots[step]] if step < 4 else [zslots[4]]
        for s in got:
            send(pf.at[s, top], pf.at[s, top], pcs.at[n], pcr.at[s], core)
            n += 1
        for s in got:
            update = update + term(s)
    o_ref[...] = (coef_a * xx[c, pl.ds(k * m, m)].astype(F32) + update).astype(BF16)
    for copy in sends:
        copy.wait_send()
    for i, b in enumerate(order):

        @pl.when(owner(b) != z)
        def _():
            src = sb.at[i] if i < EARLY else qb.at[i - EARLY]
            pltpu.make_async_remote_copy(
                src_ref=src, dst_ref=src, send_sem=zs.at[i], recv_sem=zr.at[z], device_id=core, device_id_type=MESH
            ).wait_send()

    @pl.when(mine_early)
    def _():
        for d in (1, 3, 2):
            pltpu.make_async_remote_copy(
                src_ref=eb.at[quarter(at_y(d))], dst_ref=yb.at[NB - EARLY, yh], send_sem=ys.at[NB - EARLY, d],
                recv_sem=yr.at[NB - EARLY, yh], device_id=core, device_id_type=MESH,
            ).wait_send()


def local(momentum):
    m, w = momentum.shape
    h = w // 2
    q = -(-h // (16 * NY)) * 16
    dma = lambda *n: pltpu.SemaphoreType.DMA(n)
    return pl.pallas_call(
        kernel,
        out_shape=jax.ShapeDtypeStruct((m, w), BF16),
        in_specs=[pl.BlockSpec(memory_space=pl.ANY)],
        out_specs=pl.BlockSpec(memory_space=pltpu.VMEM),
        scratch_shapes=[
            pltpu.VMEM((NB, 2 * m, w), BF16),
            pltpu.VMEM((NB, NY * q, w), BF16),
            pltpu.VMEM((NZ, NY * q, w), BF16),
            pltpu.VMEM((NY * q, w), BF16),
            pltpu.VMEM((NB - EARLY + 1, NY, q, w), BF16),
            pltpu.VMEM((NB - EARLY, q, w), BF16),
            pltpu.VMEM((NZ, q, w), BF16),
            pltpu.VMEM((q, w), F32),
            pltpu.VMEM((NZ, NY * q, w), BF16),
            pltpu.VMEM((NB, w, w), BF16),
            pltpu.VMEM((NZ, w, w), BF16),
            pltpu.VMEM((NY * q, 2 * m), BF16),
            pltpu.SemaphoreType.DMA,
            dma(2), dma(2), dma(2, 2, 2), dma(8, 2), dma(2, 2, 2), dma(8, 2), dma(3), dma(8), dma(8), dma(8),
            dma(8), dma(8), dma(8), dma(NB - EARLY + 1, 4), dma(NB - EARLY + 1, 4), dma(4), dma(4),
            dma(4, 2, 2), dma(8, 2), dma(2), dma(2), dma(2, 2, 2), dma(2, 2, 2), dma(8, 2), dma(8), dma(8),
            dma(4, 2, 2), dma(8, 2), dma(8), dma(8),
        ],
        compiler_params=pltpu.CompilerParams(
            collective_id=0, has_side_effects=True, vmem_limit_bytes=48 << 20
        ),
        name="newton_schulz",
    )(momentum)


def solution(mesh):
    return jax.shard_map(
        local,
        mesh=mesh,
        in_specs=(P("rows", "cols"),),
        out_specs=P("rows", "cols"),
        check_vma=False,
    )
```

```python
import jax
import jax.numpy as jnp
from jax import lax
from jax.experimental import pallas as pl
from jax.experimental.pallas import tpu as pltpu
from jax.sharding import PartitionSpec as P

ROWS = 25600

coef_a = 3.4445
coef_b = -4.775
coef_c = 2.0315

NZ, NY, NX = 8, 4, 4
NB = 8
EARLY = 4
UP = 208
MESH = pl.DeviceIdType.MESH
F32, BF16 = jnp.float32, jnp.bfloat16


def kernel(
    x_hbm, o_ref, xx, sb, rb, eb, yb, qb, zb, tot, gl, gr, pf, lt,
    loc, xs, cs, zs, zqs, ys, es, as_, gzs, gxs, gcs, pzs, pcs,
    wr, xr, xr2, vyr, cr, zr, zqr, yr, ar, gzr, gyr, gxr, gcr, pzr, pcr,
):
    m, w = x_hbm.shape
    h = w // 2
    q = qb.shape[1]
    hp = NY * q
    cut = -(-h // 32) * 16
    mid = -(-m // 32) * 16
    up = UP
    qtr = -(-up // 32) * 16
    r, c = lax.axis_index("rows"), lax.axis_index("cols")
    z, yh, k = r // (NY * 2), lax.rem(r // 2, NY), lax.rem(r, 2)
    yl, x = c // NX, lax.rem(c, NX)

    def rid(z=z, yh=yh, k=k):
        return (z * NY + yh) * 2 + k

    def cid(yl=yl, x=x):
        return yl * NX + x

    def at_x(d):
        return lax.rem(x + d, NX)

    def at_z(d):
        return lax.rem(z + d, NZ)

    def at_y(d):
        return lax.rem(yh + d, NY)

    core = (rid(k=1 - k), c)
    ypair = (r, cid(yl=1 - yl))
    xdev = [(r, cid(x=at_x(d))) for d in range(NX)]
    zdev = [(rid(z=at_z(d)), c) for d in range(NZ)]
    ydev = [(rid(yh=at_y(d)), c) for d in range(NY)]

    def copy(src, dst, ss, rs, to):
        return pltpu.make_async_remote_copy(
            src_ref=src, dst_ref=dst, send_sem=ss, recv_sem=rs, device_id=to, device_id_type=MESH
        )

    def send(src, dst, ss, rs, to):
        copy(src, dst, ss, rs, to).start()

    def arrived(dst, rs):
        copy(dst, dst, loc, rs, core).wait_recv()

    def sent(src, ss):
        copy(src, src, ss, loc, core).wait_send()

    mine = xx.at[c, pl.ds(k * m, m)]
    own = pltpu.make_async_copy(x_hbm, mine, loc)
    own.start()
    barrier = pltpu.get_barrier_semaphore()
    partners = [core, ypair] + xdev[1:] + zdev[1:] + ydev[1:]
    for to in partners:
        pl.semaphore_signal(barrier, inc=1, device_id=to, device_id_type=MESH)
    pl.semaphore_wait(barrier, len(partners))
    own.wait()

    xslots = [cid(x=at_x(d)) for d in range(NX)]
    xslots2 = [cid(yl=1 - yl, x=at_x(d)) for d in range(NX)]
    zslots = [at_z(d) for d in range(NZ)]
    order = [xslots[0], xslots2[0]] + [xslots[d] for d in (1, 3, 2)] + [xslots2[d] for d in (1, 3, 2)]
    c2 = order[1]

    def owner(b):
        return lax.rem(b, NX) * 2 + b // NX

    def block(s):
        return s % 2 * NX + s // 2 if isinstance(s, int) else lax.rem(s, 2) * NX + s // 2

    def ring_hop(buf, ss, rs, dev, slots, hop, right, n):
        reach = len(slots) // 2 - (right == n)
        if hop > reach:
            return
        s = slots[-hop if right else hop] if hop else slots[0]
        if hop:
            arrived(buf(s, n), rs(s, n))
        if hop < reach:
            send(buf(s, n), buf(s, n), ss, rs(s, n), dev[1 if right else -1])

    def ring_step(*args):
        for right, n in ((1, 0), (0, 1), (1, 1), (0, 0)):
            ring_hop(*args, right, n)

    def half(b):
        return xx.at[b, pl.ds(k * m, m)]

    def other(b):
        return xx.at[b, pl.ds((1 - k) * m, m)]

    def x_half(b, n):
        return xx.at[b, pl.ds(k * m + n * mid, m - mid if n else mid)]

    def x_quarter(b, n):
        return xx.at[b, pl.ds(k * m + n * qtr, up - qtr if n else qtr)]

    def x_rest(i):
        return xx.at[order[i], pl.ds(k * m + up, m - up)]

    def over(i):
        send(x_rest(i), x_rest(i), xs, vyr.at[lax.rem(order[i], NX)], ypair)

    def back(i):
        arrived(x_rest(i), vyr.at[lax.rem(order[i], NX)])

    def hand(i):
        send(half(order[i]), half(order[i]), cs, cr.at[order[i]], core)

    def quarter(p):
        return pl.ds(pl.multiple_of(p * q, q), q)

    def to_owner(i, src, dst, ss, rs):
        to = owner(order[i])

        @pl.when(to != z)
        def _():
            send(src, dst.at[z], ss, rs, (rid(z=to), c))

        @pl.when(to == z)
        def _():
            dst[z] = src[...]

    def add_up(buf, out):
        value = buf[0].astype(F32)
        for s in range(1, buf.shape[0]):
            value = value + buf[s].astype(F32)
        out[...] = value.astype(out.dtype)

    def partial(i):
        b = order[i]
        if i:
            arrived(other(b), cr.at[b])
        sb[i] = jnp.dot(lt[...], xx[b], preferred_element_type=F32).astype(BF16)
        if i < EARLY:
            to_owner(i, sb.at[i], rb, zs, zr)
        else:
            j = i - EARLY
            yb[j, yh] = sb[i, quarter(yh)]
            for d in (1, 3, 2):
                send(sb.at[i, quarter(at_y(d))], yb.at[j, yh], ys, yr.at[j], ydev[d])

    def late(i):
        j = i - EARLY
        arrived(yb.at[j, pl.ds(0, NY - 1)], yr.at[j])
        add_up(yb.at[j], qb.at[j])
        to_owner(i, qb.at[j], zb, zqs, zqr)

    rring = (x_half, xs, lambda b, n: xr.at[lax.rem(b, NX), n], xdev, xslots)
    rring2 = (x_quarter, xs, lambda b, n: xr2.at[lax.rem(b, NX), n], xdev, xslots2)
    send(half(c), half(c), xs, wr, ypair)
    ring_step(*rring, 0)
    hand(0)
    pick = (
        lax.broadcasted_iota(jnp.int32, (hp, w), 1) == lax.broadcasted_iota(jnp.int32, (hp, w), 0) + k * h
    ).astype(BF16)
    arrived(other(c), cr.at[c])
    lt[...] = lax.dot_general(
        pick, xx[c], (((1,), (1,)), ((), ())), preferred_element_type=F32
    ).astype(BF16)
    partial(0)
    arrived(half(c2), wr)
    hand(1)
    ring_step(*rring, 1)
    over(2)
    over(3)
    hand(2)
    hand(3)
    ring_step(*rring2, 0)
    partial(1)
    partial(2)
    partial(3)
    ring_step(*rring, 2)
    over(4)
    hand(4)
    ring_step(*rring2, 1)
    for i in (5, 6):
        back(i)
        hand(i)
    partial(4)
    partial(5)
    partial(6)
    ring_step(*rring2, 2)
    back(7)
    hand(7)
    partial(7)
    for i in range(EARLY, NB):
        late(i)

    mine_early = owner(order[0]) == z
    for i in range(1, EARLY):
        mine_early = jnp.logical_or(mine_early, owner(order[i]) == z)

    @pl.when(mine_early)
    def _():
        arrived(rb.at[pl.ds(0, NZ - 1)], zr)
        add_up(rb, eb)
        yb[NB - EARLY, yh] = eb[quarter(yh)]
        for d in (1, 3, 2):
            send(eb.at[quarter(at_y(d))], yb.at[NB - EARLY, yh], es, yr.at[NB - EARLY], ydev[d])
        arrived(yb.at[NB - EARLY, pl.ds(0, NY - 1)], yr.at[NB - EARLY])
        add_up(yb.at[NB - EARLY], tot)

    @pl.when(jnp.logical_not(mine_early))
    def _():
        arrived(zb.at[pl.ds(0, NZ - 1)], zqr)
        add_up(zb, tot)

    gl[z, quarter(yh)] = (tot[...] / ROWS).astype(BF16)
    for d in (1, 3, 2):
        g = gl.at[z, quarter(yh)]
        send(g, g, as_, ar, ydev[d])
    arrived(gl.at[z, pl.ds(0, hp - q)], ar)
    top = pl.ds(k * h, h)
    low = pl.ds((1 - k) * h, h)
    gram = gl[z, pl.ds(0, h)]
    gr[c, top, :] = gram

    def part(base, n):
        return pl.ds(base + n * cut, h - cut if n else cut)

    def g_row(s, n):
        return gl.at[s, part(0, n)]

    def g_col(b, n):
        return gr.at[b, part(k * h, n)]

    def p_row(s, n):
        return pf.at[s, part(k * h, n)]

    zring = (g_row, gzs, lambda s, n: gzr.at[s, n], zdev, zslots)
    xring = (g_col, gxs, lambda s, n: gxr.at[s, n], xdev, xslots)
    xring2 = (g_col, gxs, lambda s, n: gxr.at[s, n], xdev, xslots2)

    def hand_on(slots):
        for b in slots:
            send(gr.at[b, top], gr.at[b, top], gcs, gcr, core)

    send(gr.at[c, top], gr.at[c, top], gxs, gyr, ypair)
    ring_step(*xring, 0)
    ring_step(*zring, 0)
    hand_on([c])
    arrived(gr.at[c2, top], gyr)
    ring_step(*xring2, 0)
    hand_on([c2])
    ring_step(*xring, 1)
    ring_step(*zring, 1)
    hand_on([xslots[1], xslots[3]])
    ring_step(*xring, 2)
    ring_step(*zring, 2)
    hand_on([xslots[2]])
    ring_step(*xring2, 1)
    hand_on([xslots2[1], xslots2[3]])
    ring_step(*zring, 3)
    ring_step(*xring2, 2)
    hand_on([xslots2[2]])
    ring_step(*zring, 4)
    arrived(gr.at[:, pl.ds(0, h)], gcr)
    square = jnp.dot(gl[0, :h], gr[block(0)], preferred_element_type=F32)
    for s in range(1, NB):
        square = square + jnp.dot(gl[s, :h], gr[block(s)], preferred_element_type=F32)
    pf[z, top, :] = (coef_b * gram.astype(F32) + coef_c * square).astype(BF16)
    pring = (p_row, pzs, lambda s, n: pzr.at[s, n], zdev, zslots)

    def hand_over(slots):
        for s in slots:
            send(pf.at[s, top], pf.at[s, top], pcs, pcr.at[s], core)

    def term(s):
        arrived(pf.at[s, low], pcr.at[s])
        return lax.dot_general(
            xx[block(s), pl.ds(k * m, m)], pf[s], (((1,), (1,)), ((), ())), preferred_element_type=F32
        )

    ring_step(*pring, 0)
    hand_over([z])
    update = None
    held = [z]
    for step in range(1, 5):
        ring_step(*pring, step)
        got = [zslots[-step], zslots[step]] if step < 4 else [zslots[4]]
        hand_over(got)
        for s in held:
            update = term(s) if update is None else update + term(s)
        held = got
    for s in held:
        update = update + term(s)
    o_ref[...] = (coef_a * xx[c, pl.ds(k * m, m)].astype(F32) + update).astype(BF16)

    sent(xx.at[pl.ds(0, NB - 1), pl.ds(0, m)], xs)
    sent(xx.at[:, pl.ds(0, m)], cs)

    @pl.when(mine_early)
    def _():
        sent(sb.at[pl.ds(0, EARLY - 1)], zs)
        sent(qb, zqs)
        sent(eb.at[pl.ds(0, hp - q)], es)

    @pl.when(jnp.logical_not(mine_early))
    def _():
        sent(sb.at[pl.ds(0, EARLY)], zs)
        sent(qb.at[pl.ds(0, NB - EARLY - 1)], zqs)

    sent(yb.at[pl.ds(0, NB - EARLY), pl.ds(0, NY - 1)], ys)
    sent(gl.at[z, pl.ds(0, hp - q)], as_)
    sent(gl.at[pl.ds(0, NZ - 1), pl.ds(0, h)], gzs)
    sent(gr.at[pl.ds(0, NB - 1), pl.ds(0, h)], gxs)
    sent(gr.at[:, pl.ds(0, h)], gcs)
    sent(pf.at[pl.ds(0, NZ - 1), pl.ds(0, h)], pzs)
    sent(pf.at[:, pl.ds(0, h)], pcs)


def local(momentum):
    m, w = momentum.shape
    h = w // 2
    q = -(-h // (16 * NY)) * 16
    dma = lambda *n: pltpu.SemaphoreType.DMA(n)
    one = pltpu.SemaphoreType.DMA
    return pl.pallas_call(
        kernel,
        out_shape=jax.ShapeDtypeStruct((m, w), BF16),
        in_specs=[pl.BlockSpec(memory_space=pl.ANY)],
        out_specs=pl.BlockSpec(memory_space=pltpu.VMEM),
        scratch_shapes=[
            pltpu.VMEM((NB, 2 * m, w), BF16),
            pltpu.VMEM((NB, NY * q, w), BF16),
            pltpu.VMEM((NZ, NY * q, w), BF16),
            pltpu.VMEM((NY * q, w), BF16),
            pltpu.VMEM((NB - EARLY + 1, NY, q, w), BF16),
            pltpu.VMEM((NB - EARLY, q, w), BF16),
            pltpu.VMEM((NZ, q, w), BF16),
            pltpu.VMEM((q, w), F32),
            pltpu.VMEM((NZ, NY * q, w), BF16),
            pltpu.VMEM((NB, w, w), BF16),
            pltpu.VMEM((NZ, w, w), BF16),
            pltpu.VMEM((NY * q, 2 * m), BF16),
            one, one, one, one, one, one, one, one, one, one, one, one, one,
            one, dma(NX, 2), dma(NX, 2), dma(NX), dma(NB), one, one, dma(NB - EARLY + 1), one,
            dma(NZ, 2), one, dma(NB, 2), one, dma(NZ, 2), dma(NZ),
        ],
        compiler_params=pltpu.CompilerParams(
            collective_id=0, has_side_effects=True, vmem_limit_bytes=48 << 20
        ),
        name="newton_schulz",
    )(momentum)


def solution(mesh):
    return jax.shard_map(
        local,
        mesh=mesh,
        in_specs=(P("rows", "cols"),),
        out_specs=P("rows", "cols"),
        check_vma=False,
    )
```

```python
import jax
import jax.numpy as jnp
from jax import lax
from jax.experimental import pallas as pl
from jax.experimental.pallas import tpu as pltpu
from jax.sharding import PartitionSpec as P

ROWS = 25600

coef_a = 3.4445
coef_b = -4.775
coef_c = 2.0315

NZ, NY, NX = 8, 4, 4
NB = 8
EARLY = 4
UP = 256
MESH = pl.DeviceIdType.MESH
F32, BF16 = jnp.float32, jnp.bfloat16


def kernel(
    x_hbm, o_ref, xx, sb, rb, eb, yb, qb, zb, tot, gl, gr, pf, lt,
    loc, xs, cs, zs, zqs, ys, es, as_, gzs, gxs, gcs, pzs, pcs,
    wr, xr, xr2, vyr, cr, zr, zqr, yr, ar, gzr, gyr, gxr, gcr, pzr, pcr,
):
    m, w = x_hbm.shape
    h = w // 2
    q = qb.shape[1]
    hp = NY * q
    cut = -(-h // 32) * 16
    mid = -(-m // 32) * 16
    up = UP
    qtr = -(-up // 32) * 16
    r, c = lax.axis_index("rows"), lax.axis_index("cols")
    z, yh, k = r // (NY * 2), lax.rem(r // 2, NY), lax.rem(r, 2)
    yl, x = c // NX, lax.rem(c, NX)

    def rid(z=z, yh=yh, k=k):
        return (z * NY + yh) * 2 + k

    def cid(yl=yl, x=x):
        return yl * NX + x

    def at_x(d):
        return lax.rem(x + d, NX)

    def at_z(d):
        return lax.rem(z + d, NZ)

    def at_y(d):
        return lax.rem(yh + d, NY)

    core = (rid(k=1 - k), c)
    ypair = (r, cid(yl=1 - yl))
    xdev = [(r, cid(x=at_x(d))) for d in range(NX)]
    zdev = [(rid(z=at_z(d)), c) for d in range(NZ)]
    ydev = [(rid(yh=at_y(d)), c) for d in range(NY)]

    def copy(src, dst, ss, rs, to):
        return pltpu.make_async_remote_copy(
            src_ref=src, dst_ref=dst, send_sem=ss, recv_sem=rs, device_id=to, device_id_type=MESH
        )

    def send(src, dst, ss, rs, to):
        copy(src, dst, ss, rs, to).start()

    def arrived(dst, rs):
        copy(dst, dst, loc, rs, core).wait_recv()

    def sent(src, ss):
        copy(src, src, ss, loc, core).wait_send()

    mine = xx.at[c, pl.ds(k * m, m)]
    own = pltpu.make_async_copy(x_hbm, mine, loc)
    own.start()
    barrier = pltpu.get_barrier_semaphore()
    partners = [core, ypair] + xdev[1:] + [(r, cid(yl=1 - yl, x=at_x(d))) for d in (1, 2, 3)] + zdev[1:] + ydev[1:]
    for to in partners:
        pl.semaphore_signal(barrier, inc=1, device_id=to, device_id_type=MESH)
    pl.semaphore_wait(barrier, len(partners))
    own.wait()

    xslots = [cid(x=at_x(d)) for d in range(NX)]
    xslots2 = [cid(yl=1 - yl, x=at_x(d)) for d in range(NX)]
    zslots = [at_z(d) for d in range(NZ)]
    order = [xslots[0], xslots2[0]] + [xslots[d] for d in (1, 3, 2)] + [xslots2[d] for d in (1, 3, 2)]
    c2 = order[1]

    def owner(b):
        return lax.rem(b, NX) * 2 + b // NX

    def block(s):
        return s % 2 * NX + s // 2 if isinstance(s, int) else lax.rem(s, 2) * NX + s // 2

    def ring_hop(buf, ss, rs, dev, slots, hop, right, n):
        reach = len(slots) // 2 - (right == n)
        if hop > reach:
            return
        s = slots[-hop if right else hop] if hop else slots[0]
        if hop:
            arrived(buf(s, n), rs(s, n))
        if hop < reach:
            send(buf(s, n), buf(s, n), ss, rs(s, n), dev[1 if right else -1])

    def ring_step(*args):
        for right, n in ((1, 0), (0, 1), (1, 1), (0, 0)):
            ring_hop(*args, right, n)

    def half(b):
        return xx.at[b, pl.ds(k * m, m)]

    def other(b):
        return xx.at[b, pl.ds((1 - k) * m, m)]

    def x_half(b, n):
        return xx.at[b, pl.ds(k * m + n * mid, m - mid if n else mid)]

    def x_quarter(b, n):
        return xx.at[b, pl.ds(k * m + n * qtr, up - qtr if n else qtr)]

    def x_rest(i):
        return xx.at[order[i], pl.ds(k * m + up, m - up)]

    def over(i):
        send(x_rest(i), x_rest(i), xs, vyr.at[lax.rem(order[i], NX)], ypair)

    def back(i):
        arrived(x_rest(i), vyr.at[lax.rem(order[i], NX)])

    def hand(i):
        send(half(order[i]), half(order[i]), cs, cr.at[order[i]], core)

    def quarter(p):
        return pl.ds(pl.multiple_of(p * q, q), q)

    def to_owner(i, src, dst, ss, rs):
        to = owner(order[i])

        @pl.when(to != z)
        def _():
            send(src, dst.at[z], ss, rs, (rid(z=to), c))

        @pl.when(to == z)
        def _():
            dst[z] = src[...]

    def add_up(buf, out):
        value = buf[0].astype(F32)
        for s in range(1, buf.shape[0]):
            value = value + buf[s].astype(F32)
        out[...] = value.astype(out.dtype)

    def partial(i):
        b = order[i]
        if i:
            arrived(other(b), cr.at[b])
        sb[i] = jnp.dot(lt[...], xx[b], preferred_element_type=F32).astype(BF16)
        if i < EARLY:
            to_owner(i, sb.at[i], rb, zs, zr)
        else:
            j = i - EARLY
            yb[j, yh] = sb[i, quarter(yh)]
            for d in (1, 3, 2):
                send(sb.at[i, quarter(at_y(d))], yb.at[j, yh], ys, yr.at[j], ydev[d])

    def late(i):
        j = i - EARLY
        arrived(yb.at[j, pl.ds(0, NY - 1)], yr.at[j])
        add_up(yb.at[j], qb.at[j])
        to_owner(i, qb.at[j], zb, zqs, zqr)

    rring = (x_half, xs, lambda b, n: xr.at[lax.rem(b, NX), n], xdev, xslots)
    rring2 = (x_quarter, xs, lambda b, n: xr2.at[lax.rem(b, NX), n], xdev, xslots2)
    send(half(c), half(c), xs, wr, ypair)
    ring_step(*rring, 0)
    hand(0)
    pick = (
        lax.broadcasted_iota(jnp.int32, (hp, w), 1) == lax.broadcasted_iota(jnp.int32, (hp, w), 0) + k * h
    ).astype(BF16)
    arrived(other(c), cr.at[c])
    lt[...] = lax.dot_general(
        pick, xx[c], (((1,), (1,)), ((), ())), preferred_element_type=F32
    ).astype(BF16)
    partial(0)
    ring_step(*rring, 1)
    over(2)
    over(3)
    hand(2)
    hand(3)
    arrived(half(c2), wr)
    ring_step(*rring2, 0)
    hand(1)
    partial(1)
    partial(2)
    partial(3)
    ring_step(*rring, 2)
    over(4)
    hand(4)
    ring_step(*rring2, 1)
    for i in (5, 6):
        back(i)
        hand(i)
    partial(4)
    partial(5)
    partial(6)
    ring_step(*rring2, 2)
    back(7)
    hand(7)
    partial(7)
    mine_early = owner(order[0]) == z
    for i in range(1, EARLY):
        mine_early = jnp.logical_or(mine_early, owner(order[i]) == z)

    @pl.when(mine_early)
    def _():
        arrived(rb.at[pl.ds(0, NZ - 1)], zr)
        add_up(rb, eb)
        yb[NB - EARLY, yh] = eb[quarter(yh)]
        for d in (1, 3, 2):
            send(eb.at[quarter(at_y(d))], yb.at[NB - EARLY, yh], es, yr.at[NB - EARLY], ydev[d])

    for i in range(EARLY, NB):
        late(i)

    @pl.when(mine_early)
    def _():
        arrived(yb.at[NB - EARLY, pl.ds(0, NY - 1)], yr.at[NB - EARLY])
        add_up(yb.at[NB - EARLY], tot)

    @pl.when(jnp.logical_not(mine_early))
    def _():
        arrived(zb.at[pl.ds(0, NZ - 1)], zqr)
        add_up(zb, tot)

    gl[z, quarter(yh)] = (tot[...] / ROWS).astype(BF16)
    for d in (1, 3, 2):
        g = gl.at[z, quarter(yh)]
        send(g, g, as_, ar, ydev[d])
    arrived(gl.at[z, pl.ds(0, hp - q)], ar)
    top = pl.ds(k * h, h)
    low = pl.ds((1 - k) * h, h)
    gram = gl[z, pl.ds(0, h)]
    gr[c, top, :] = gram

    def part(base, n):
        return pl.ds(base + n * cut, h - cut if n else cut)

    def g_row(s, n):
        return gl.at[s, part(0, n)]

    def g_col(b, n):
        return gr.at[b, part(k * h, n)]

    def p_row(s, n):
        return pf.at[s, part(k * h, n)]

    zring = (g_row, gzs, lambda s, n: gzr.at[s, n], zdev, zslots)
    xring = (g_col, gxs, lambda s, n: gxr.at[s, n], xdev, xslots)
    xring2 = (g_col, gxs, lambda s, n: gxr.at[s, n], xdev, xslots2)

    def hand_on(slots):
        for b in slots:
            send(gr.at[b, top], gr.at[b, top], gcs, gcr, core)

    for to in [ypair] + [xdev[d] for d in (1, 3, 2)] + [(r, xslots2[d]) for d in (1, 3, 2)]:
        send(gr.at[c, top], gr.at[c, top], gxs, gxr.at[c, 0], to)
    ring_step(*zring, 0)
    hand_on([c])
    ring_step(*zring, 1)
    ring_step(*zring, 2)
    for b in order[1:5]:
        arrived(gr.at[b, top], gxr.at[b, 0])
        hand_on([b])
    ring_step(*zring, 3)
    for b in order[5:]:
        arrived(gr.at[b, top], gxr.at[b, 0])
        hand_on([b])
    ring_step(*zring, 4)
    arrived(gr.at[:, pl.ds(0, h)], gcr)
    square = jnp.dot(gl[0, :h], gr[block(0)], preferred_element_type=F32)
    for s in range(1, NB):
        square = square + jnp.dot(gl[s, :h], gr[block(s)], preferred_element_type=F32)
    pf[z, top, :] = (coef_b * gram.astype(F32) + coef_c * square).astype(BF16)
    pring = (p_row, pzs, lambda s, n: pzr.at[s, n], zdev, zslots)

    def hand_over(slots):
        for s in slots:
            send(pf.at[s, top], pf.at[s, top], pcs, pcr.at[s], core)

    def term(s):
        arrived(pf.at[s, low], pcr.at[s])
        return lax.dot_general(
            xx[block(s), pl.ds(k * m, m)], pf[s], (((1,), (1,)), ((), ())), preferred_element_type=F32
        )

    ring_step(*pring, 0)
    hand_over([z])
    update = None
    held = [z]
    for step in range(1, 5):
        ring_step(*pring, step)
        got = [zslots[-step], zslots[step]] if step < 4 else [zslots[4]]
        hand_over(got)
        for s in held:
            update = term(s) if update is None else update + term(s)
        held = got
    for s in held:
        update = update + term(s)
    o_ref[...] = (coef_a * xx[c, pl.ds(k * m, m)].astype(F32) + update).astype(BF16)

    sent(xx.at[pl.ds(0, NB - 1), pl.ds(0, m)], xs)
    sent(xx.at[:, pl.ds(0, m)], cs)

    @pl.when(mine_early)
    def _():
        sent(sb.at[pl.ds(0, EARLY - 1)], zs)
        sent(qb, zqs)
        sent(eb.at[pl.ds(0, hp - q)], es)

    @pl.when(jnp.logical_not(mine_early))
    def _():
        sent(sb.at[pl.ds(0, EARLY)], zs)
        sent(qb.at[pl.ds(0, NB - EARLY - 1)], zqs)

    sent(yb.at[pl.ds(0, NB - EARLY), pl.ds(0, NY - 1)], ys)
    sent(gl.at[z, pl.ds(0, hp - q)], as_)
    sent(gl.at[pl.ds(0, NZ - 1), pl.ds(0, h)], gzs)
    sent(gr.at[pl.ds(0, NB - 1), pl.ds(0, h)], gxs)
    sent(gr.at[:, pl.ds(0, h)], gcs)
    sent(pf.at[pl.ds(0, NZ - 1), pl.ds(0, h)], pzs)
    sent(pf.at[:, pl.ds(0, h)], pcs)


def local(momentum):
    m, w = momentum.shape
    h = w // 2
    q = -(-h // (16 * NY)) * 16
    dma = lambda *n: pltpu.SemaphoreType.DMA(n)
    one = pltpu.SemaphoreType.DMA
    return pl.pallas_call(
        kernel,
        out_shape=jax.ShapeDtypeStruct((m, w), BF16),
        in_specs=[pl.BlockSpec(memory_space=pl.ANY)],
        out_specs=pl.BlockSpec(memory_space=pltpu.VMEM),
        scratch_shapes=[
            pltpu.VMEM((NB, 2 * m, w), BF16),
            pltpu.VMEM((NB, NY * q, w), BF16),
            pltpu.VMEM((NZ, NY * q, w), BF16),
            pltpu.VMEM((NY * q, w), BF16),
            pltpu.VMEM((NB - EARLY + 1, NY, q, w), BF16),
            pltpu.VMEM((NB - EARLY, q, w), BF16),
            pltpu.VMEM((NZ, q, w), BF16),
            pltpu.VMEM((q, w), F32),
            pltpu.VMEM((NZ, NY * q, w), BF16),
            pltpu.VMEM((NB, w, w), BF16),
            pltpu.VMEM((NZ, w, w), BF16),
            pltpu.VMEM((NY * q, 2 * m), BF16),
            one, one, one, one, one, one, one, one, one, one, one, one, one,
            one, dma(NX, 2), dma(NX, 2), dma(NX), dma(NB), one, one, dma(NB - EARLY + 1), one,
            dma(NZ, 2), one, dma(NB, 2), one, dma(NZ, 2), dma(NZ),
        ],
        compiler_params=pltpu.CompilerParams(
            collective_id=0, has_side_effects=True, vmem_limit_bytes=48 << 20
        ),
        name="newton_schulz",
    )(momentum)


def solution(mesh):
    return jax.shard_map(
        local,
        mesh=mesh,
        in_specs=(P("rows", "cols"),),
        out_specs=P("rows", "cols"),
        check_vma=False,
    )
```

```python
import jax
import jax.numpy as jnp
from jax import lax
from jax.experimental import pallas as pl
from jax.experimental.pallas import tpu as pltpu
from jax.sharding import PartitionSpec as P

ROWS = 25600

coef_a = 3.4445
coef_b = -4.775
coef_c = 2.0315

NZ, NY, NX = 8, 4, 4
NB = 8
EARLY = 4
UP = 256
MESH = pl.DeviceIdType.MESH
F32, BF16 = jnp.float32, jnp.bfloat16


def kernel(
    x_hbm, o_ref, xx, sb, rb, eb, yb, qb, zb, tot, gl, gr, pf, lt,
    loc, xs, cs, zs, zqs, ys, es, as_, gzs, gxs, gcs, pzs, pcs,
    wr, xr, xr2, vyr, cr, zr, zqr, yr, ar, gzr, gxr, gcr, pzr, pcr,
):
    m, w = x_hbm.shape
    h = w // 2
    q = qb.shape[1]
    hp = NY * q
    ql = h - (NY - 1) * q
    cut = -(-h // 32) * 16
    mid = -(-m // 32) * 16
    up = UP
    qtr = -(-up // 32) * 16
    r, c = lax.axis_index("rows"), lax.axis_index("cols")
    z, yh, k = r // (NY * 2), lax.rem(r // 2, NY), lax.rem(r, 2)
    yl, x = c // NX, lax.rem(c, NX)

    def rid(z=z, yh=yh, k=k):
        return (z * NY + yh) * 2 + k

    def cid(yl=yl, x=x):
        return yl * NX + x

    def at_x(d):
        return lax.rem(x + d, NX)

    def at_z(d):
        return lax.rem(z + d, NZ)

    def at_y(d):
        return lax.rem(yh + d, NY)

    core = (rid(k=1 - k), c)
    ypair = (r, cid(yl=1 - yl))
    xdev = [(r, cid(x=at_x(d))) for d in range(NX)]
    zdev = [(rid(z=at_z(d)), c) for d in range(NZ)]
    ydev = [(rid(yh=at_y(d)), c) for d in range(NY)]

    def copy(src, dst, ss, rs, to):
        return pltpu.make_async_remote_copy(
            src_ref=src, dst_ref=dst, send_sem=ss, recv_sem=rs, device_id=to, device_id_type=MESH
        )

    def send(src, dst, ss, rs, to):
        copy(src, dst, ss, rs, to).start()

    def arrived(dst, rs):
        copy(dst, dst, loc, rs, core).wait_recv()

    def sent(src, ss):
        copy(src, src, ss, loc, core).wait_send()

    mine = xx.at[c, pl.ds(k * m, m)]
    own = pltpu.make_async_copy(x_hbm, mine, loc)
    own.start()
    barrier = pltpu.get_barrier_semaphore()
    partners = [core, ypair] + xdev[1:] + [(r, cid(yl=1 - yl, x=at_x(d))) for d in (1, 2, 3)] + zdev[1:] + ydev[1:]
    for to in partners:
        pl.semaphore_signal(barrier, inc=1, device_id=to, device_id_type=MESH)
    pl.semaphore_wait(barrier, len(partners))
    own.wait()

    xslots = [cid(x=at_x(d)) for d in range(NX)]
    xslots2 = [cid(yl=1 - yl, x=at_x(d)) for d in range(NX)]
    zslots = [at_z(d) for d in range(NZ)]
    order = [xslots[0], xslots2[0]] + [xslots[d] for d in (1, 3, 2)] + [xslots2[d] for d in (1, 3, 2)]
    c2 = order[1]

    def owner(b):
        return lax.rem(b, NX) * 2 + b // NX

    def block(s):
        return s % 2 * NX + s // 2 if isinstance(s, int) else lax.rem(s, 2) * NX + s // 2

    def ring_hop(buf, ss, rs, dev, slots, hop, right, n):
        reach = len(slots) // 2 - (right == n)
        if hop > reach:
            return
        s = slots[-hop if right else hop] if hop else slots[0]
        if hop:
            arrived(buf(s, n), rs(s, n))
        if hop < reach:
            send(buf(s, n), buf(s, n), ss, rs(s, n), dev[1 if right else -1])

    def ring_step(*args):
        for right, n in ((1, 0), (0, 1), (1, 1), (0, 0)):
            ring_hop(*args, right, n)

    def half(b):
        return xx.at[b, pl.ds(k * m, m)]

    def other(b):
        return xx.at[b, pl.ds((1 - k) * m, m)]

    def x_half(b, n):
        return xx.at[b, pl.ds(k * m + n * mid, m - mid if n else mid)]

    def x_quarter(b, n):
        return xx.at[b, pl.ds(k * m + n * qtr, up - qtr if n else qtr)]

    def x_rest(i):
        return xx.at[order[i], pl.ds(k * m + up, m - up)]

    def over(i):
        send(x_rest(i), x_rest(i), xs, vyr.at[lax.rem(order[i], NX)], ypair)

    def back(i):
        arrived(x_rest(i), vyr.at[lax.rem(order[i], NX)])

    def hand(i):
        send(half(order[i]), half(order[i]), cs, cr.at[order[i]], core)

    def quarter(p):
        return pl.ds(pl.multiple_of(p * q, q), q)

    def with_quarter(p, do):
        @pl.when(p < NY - 1)
        def _():
            do(quarter(p), q)

        @pl.when(p == NY - 1)
        def _():
            do(pl.ds((NY - 1) * q, ql), ql)

    def spread(src, dst, ss, rs):
        for d in (1, 3, 2):
            with_quarter(at_y(d), lambda rows, n: send(src.at[rows], dst.at[yh, pl.ds(0, n)], ss, rs, ydev[d]))

    def quarters_in(buf, rs):
        with_quarter(yh, lambda rows, n: arrived(buf.at[pl.ds(0, NY - 1), pl.ds(0, n)], rs))

    def to_owner(i, src, dst, ss, rs):
        to = owner(order[i])

        @pl.when(to != z)
        def _():
            send(src, dst.at[z], ss, rs, (rid(z=to), c))

        @pl.when(to == z)
        def _():
            dst[z] = src[...]

    def add_up(buf, out):
        value = buf[0].astype(F32)
        for s in range(1, buf.shape[0]):
            value = value + buf[s].astype(F32)
        out[...] = value.astype(out.dtype)

    def partial(i):
        b = order[i]
        if i:
            arrived(other(b), cr.at[b])
        sb[i] = jnp.dot(lt[...], xx[b], preferred_element_type=F32).astype(BF16)
        if i < EARLY:
            to_owner(i, sb.at[i], rb, zs, zr)
        else:
            j = i - EARLY
            yb[j, yh] = sb[i, quarter(yh)]
            spread(sb.at[i], yb.at[j], ys, yr.at[j])

    def late(i):
        j = i - EARLY
        quarters_in(yb.at[j], yr.at[j])
        add_up(yb.at[j], qb.at[j])
        to_owner(i, qb.at[j], zb, zqs, zqr)

    rring = (x_half, xs, lambda b, n: xr.at[lax.rem(b, NX), n], xdev, xslots)
    rring2 = (x_quarter, xs, lambda b, n: xr2.at[lax.rem(b, NX), n], xdev, xslots2)
    send(half(c), half(c), xs, wr, ypair)
    ring_step(*rring, 0)
    hand(0)
    pick = (
        lax.broadcasted_iota(jnp.int32, (hp, w), 1) == lax.broadcasted_iota(jnp.int32, (hp, w), 0) + k * h
    ).astype(BF16)
    arrived(other(c), cr.at[c])
    lt[...] = lax.dot_general(
        pick, xx[c], (((1,), (1,)), ((), ())), preferred_element_type=F32
    ).astype(BF16)
    partial(0)
    ring_step(*rring, 1)
    over(2)
    over(3)
    hand(2)
    hand(3)
    arrived(half(c2), wr)
    ring_step(*rring2, 0)
    hand(1)
    partial(1)
    partial(2)
    partial(3)
    ring_step(*rring, 2)
    over(4)
    hand(4)
    ring_step(*rring2, 1)
    for i in (5, 6):
        back(i)
        hand(i)
    partial(4)
    partial(5)
    partial(6)
    ring_step(*rring2, 2)
    back(7)
    hand(7)
    partial(7)
    mine_early = owner(order[0]) == z
    for i in range(1, EARLY):
        mine_early = jnp.logical_or(mine_early, owner(order[i]) == z)

    @pl.when(mine_early)
    def _():
        arrived(rb.at[pl.ds(0, NZ - 1)], zr)
        add_up(rb, eb)
        yb[NB - EARLY, yh] = eb[quarter(yh)]
        spread(eb, yb.at[NB - EARLY], es, yr.at[NB - EARLY])

    for i in range(EARLY, NB):
        late(i)

    @pl.when(mine_early)
    def _():
        quarters_in(yb.at[NB - EARLY], yr.at[NB - EARLY])
        add_up(yb.at[NB - EARLY], tot)

    @pl.when(jnp.logical_not(mine_early))
    def _():
        arrived(zb.at[pl.ds(0, NZ - 1)], zqr)
        add_up(zb, tot)

    top = pl.ds(k * h, h)
    low = pl.ds((1 - k) * h, h)
    columns = [ypair] + [xdev[d] for d in (1, 3, 2)] + [(r, xslots2[d]) for d in (1, 3, 2)]

    def over_z(s, rows, j, hop, right):
        if hop < NZ // 2 - (right == j % 2):
            g = gl.at[s, rows]
            send(g, g, gzs, gzr.at[s, j], zdev[1 if right else -1])

    def set_off(j):
        def go(rows, n):
            g = gl.at[z, rows]
            if j == 0:
                gl[z, rows] = (tot[pl.ds(0, n)] / ROWS).astype(BF16)
                for d in (1, 3, 2):
                    send(g, g, as_, ar.at[NY - d], ydev[d])
            else:
                arrived(g, ar.at[j])
            for right in (1, 0):
                over_z(z, rows, j, 0, right)
            for to in columns:
                send(g, gr.at[c, pl.ds(pl.multiple_of(k * h + rows.start, 16), n)], gxs, gxr.at[c], to)

        with_quarter(at_y(j), go)

    def hops(step, js):
        for j in js:
            for right in (1, 0):
                if step <= NZ // 2 - (right == j % 2):
                    s = zslots[-step if right else step]

                    def go(rows, n):
                        arrived(gl.at[s, rows], gzr.at[s, j])
                        over_z(s, rows, j, step, right)

                    with_quarter(at_y(j), go)

    def hand_on(slots):
        for b in slots:
            send(gr.at[b, top], gr.at[b, top], gcs, gcr, core)

    def columns_in(slots):
        for b in slots:
            arrived(gr.at[b, top], gxr.at[b])
            hand_on([b])

    set_off(0)
    set_off(1)
    set_off(3)
    hops(1, (0,))
    set_off(2)
    gram = gl[z]
    gr[c, top, :] = gram
    hand_on([c])
    hops(1, (1, 3))
    hops(2, (0,))
    hops(1, (2,))
    hops(2, (1, 3))
    hops(3, (0,))
    hops(2, (2,))
    columns_in(order[1:4])
    hops(3, (1, 3))
    hops(4, (0,))
    hops(3, (2,))
    columns_in(order[4:])
    hops(4, (1, 3, 2))
    arrived(gr.at[:, pl.ds(0, h)], gcr)
    square = jnp.dot(gl[0], gr[block(0)], preferred_element_type=F32)
    for s in range(1, NB):
        square = square + jnp.dot(gl[s], gr[block(s)], preferred_element_type=F32)
    pf[z, top, :] = (coef_b * gram.astype(F32) + coef_c * square).astype(BF16)
    def p_row(s, n):
        return pf.at[s, pl.ds(k * h + n * cut, h - cut if n else cut)]

    pring = (p_row, pzs, lambda s, n: pzr.at[s, n], zdev, zslots)

    def hand_over(slots):
        for s in slots:
            send(pf.at[s, top], pf.at[s, top], pcs, pcr.at[s], core)

    def term(s):
        arrived(pf.at[s, low], pcr.at[s])
        return lax.dot_general(
            xx[block(s), pl.ds(k * m, m)], pf[s], (((1,), (1,)), ((), ())), preferred_element_type=F32
        )

    ring_step(*pring, 0)
    hand_over([z])
    update = None
    held = [z]
    for step in range(1, 5):
        ring_step(*pring, step)
        got = [zslots[-step], zslots[step]] if step < 4 else [zslots[4]]
        hand_over(got)
        for s in held:
            update = term(s) if update is None else update + term(s)
        held = got
    for s in held:
        update = update + term(s)
    o_ref[...] = (coef_a * xx[c, pl.ds(k * m, m)].astype(F32) + update).astype(BF16)

    sent(xx.at[pl.ds(0, NB - 1), pl.ds(0, m)], xs)
    sent(xx.at[:, pl.ds(0, m)], cs)

    @pl.when(mine_early)
    def _():
        sent(sb.at[pl.ds(0, EARLY - 1)], zs)
        sent(qb, zqs)
        with_quarter(yh, lambda rows, n: sent(eb.at[pl.ds(0, h - n)], es))

    @pl.when(jnp.logical_not(mine_early))
    def _():
        sent(sb.at[pl.ds(0, EARLY)], zs)
        sent(qb.at[pl.ds(0, NB - EARLY - 1)], zqs)

    with_quarter(yh, lambda rows, n: sent(sb.at[pl.ds(0, NB - EARLY), pl.ds(0, h - n)], ys))
    with_quarter(yh, lambda rows, n: sent(gl.at[pl.ds(0, NY - 1), pl.ds(0, n)], as_))
    sent(gl.at[pl.ds(0, NZ - 1)], gzs)
    sent(gr.at[pl.ds(0, NB - 1), pl.ds(0, h)], gxs)
    sent(gr.at[:, pl.ds(0, h)], gcs)
    sent(pf.at[pl.ds(0, NZ - 1), pl.ds(0, h)], pzs)
    sent(pf.at[:, pl.ds(0, h)], pcs)


def local(momentum):
    m, w = momentum.shape
    h = w // 2
    q = -(-h // (16 * NY)) * 16
    dma = lambda *n: pltpu.SemaphoreType.DMA(n)
    one = pltpu.SemaphoreType.DMA
    return pl.pallas_call(
        kernel,
        out_shape=jax.ShapeDtypeStruct((m, w), BF16),
        in_specs=[pl.BlockSpec(memory_space=pl.ANY)],
        out_specs=pl.BlockSpec(memory_space=pltpu.VMEM),
        scratch_shapes=[
            pltpu.VMEM((NB, 2 * m, w), BF16),
            pltpu.VMEM((NB, NY * q, w), BF16),
            pltpu.VMEM((NZ, NY * q, w), BF16),
            pltpu.VMEM((NY * q, w), BF16),
            pltpu.VMEM((NB - EARLY + 1, NY, q, w), BF16),
            pltpu.VMEM((NB - EARLY, q, w), BF16),
            pltpu.VMEM((NZ, q, w), BF16),
            pltpu.VMEM((q, w), F32),
            pltpu.VMEM((NZ, h, w), BF16),
            pltpu.VMEM((NB, w, w), BF16),
            pltpu.VMEM((NZ, w, w), BF16),
            pltpu.VMEM((NY * q, 2 * m), BF16),
            one, one, one, one, one, one, one, one, one, one, one, one, one,
            one, dma(NX, 2), dma(NX, 2), dma(NX), dma(NB), one, one, dma(NB - EARLY + 1), dma(NY),
            dma(NZ, NY), dma(NB), one, dma(NZ, 2), dma(NZ),
        ],
        compiler_params=pltpu.CompilerParams(
            collective_id=0, has_side_effects=True, vmem_limit_bytes=48 << 20
        ),
        name="newton_schulz",
    )(momentum)


def solution(mesh):
    return jax.shard_map(
        local,
        mesh=mesh,
        in_specs=(P("rows", "cols"),),
        out_specs=P("rows", "cols"),
        check_vma=False,
    )
```

```python
import jax
import jax.numpy as jnp
from jax import lax
from jax.experimental import pallas as pl
from jax.experimental.pallas import tpu as pltpu
from jax.sharding import PartitionSpec as P

ROWS = 25600

coef_a = 3.4445
coef_b = -4.775
coef_c = 2.0315

NZ, NY, NX = 8, 4, 4
NB = 8
EARLY = 4
UP = 256
POS = 7
MESH = pl.DeviceIdType.MESH
F32, BF16 = jnp.float32, jnp.bfloat16


def kernel(
    x_hbm, o_ref, xx, sb, rb, eb, yb, qb, zb, tot, gl, gr, pf, lt,
    loc, xs, cs, zs, zqs, ys, es, as_, gzs, gxs, gcs, pzs, pcs,
    wr, xr, xr2, vyr, cr, zr, zqr, yr, ar, gzr, gxr, gcr, pzr, pcr,
):
    m, w = x_hbm.shape
    h = w // 2
    q = qb.shape[1]
    hp = NY * q
    ql = h - (NY - 1) * q
    cut = -(-h // 32) * 16
    mid = -(-m // 32) * 16
    up = UP
    qtr = -(-up // 32) * 16
    r, c = lax.axis_index("rows"), lax.axis_index("cols")
    z, yh, k = r // (NY * 2), lax.rem(r // 2, NY), lax.rem(r, 2)
    yl, x = c // NX, lax.rem(c, NX)

    def rid(z=z, yh=yh, k=k):
        return (z * NY + yh) * 2 + k

    def cid(yl=yl, x=x):
        return yl * NX + x

    def at_x(d):
        return lax.rem(x + d, NX)

    def at_z(d):
        return lax.rem(z + d, NZ)

    def at_y(d):
        return lax.rem(yh + d, NY)

    core = (rid(k=1 - k), c)
    ypair = (r, cid(yl=1 - yl))
    xdev = [(r, cid(x=at_x(d))) for d in range(NX)]
    zdev = [(rid(z=at_z(d)), c) for d in range(NZ)]
    ydev = [(rid(yh=at_y(d)), c) for d in range(NY)]

    def copy(src, dst, ss, rs, to):
        return pltpu.make_async_remote_copy(
            src_ref=src, dst_ref=dst, send_sem=ss, recv_sem=rs, device_id=to, device_id_type=MESH
        )

    def send(src, dst, ss, rs, to):
        copy(src, dst, ss, rs, to).start()

    def arrived(dst, rs):
        copy(dst, dst, loc, rs, core).wait_recv()

    def sent(src, ss):
        copy(src, src, ss, loc, core).wait_send()

    mine = xx.at[c, pl.ds(k * m, m)]
    own = pltpu.make_async_copy(x_hbm, mine, loc)
    own.start()
    barrier = pltpu.get_barrier_semaphore()
    partners = [core, ypair] + xdev[1:] + [(r, cid(yl=1 - yl, x=at_x(d))) for d in (1, 2, 3)] + zdev[1:] + ydev[1:]
    for to in partners:
        pl.semaphore_signal(barrier, inc=1, device_id=to, device_id_type=MESH)
    pl.semaphore_wait(barrier, len(partners))
    own.wait()

    xslots = [cid(x=at_x(d)) for d in range(NX)]
    xslots2 = [cid(yl=1 - yl, x=at_x(d)) for d in range(NX)]
    zslots = [at_z(d) for d in range(NZ)]
    order = [xslots[0], xslots2[0]] + [xslots[d] for d in (1, 3, 2)] + [xslots2[d] for d in (1, 3, 2)]
    c2 = order[1]

    def owner(b):
        return lax.rem(b, NX) * 2 + b // NX

    def block(s):
        return s % 2 * NX + s // 2 if isinstance(s, int) else lax.rem(s, 2) * NX + s // 2

    def ring_hop(buf, ss, rs, dev, slots, hop, right, n):
        reach = len(slots) // 2 - (right == n)
        if hop > reach:
            return
        s = slots[-hop if right else hop] if hop else slots[0]
        if hop:
            arrived(buf(s, n), rs(s, n))
        if hop < reach:
            send(buf(s, n), buf(s, n), ss, rs(s, n), dev[1 if right else -1])

    def ring_step(*args):
        for right, n in ((1, 0), (0, 1), (1, 1), (0, 0)):
            ring_hop(*args, right, n)

    def half(b):
        return xx.at[b, pl.ds(k * m, m)]

    def other(b):
        return xx.at[b, pl.ds((1 - k) * m, m)]

    def x_half(b, n):
        return xx.at[b, pl.ds(k * m + n * mid, m - mid if n else mid)]

    def x_quarter(b, n):
        return xx.at[b, pl.ds(k * m + n * qtr, up - qtr if n else qtr)]

    def x_rest(i):
        return xx.at[order[i], pl.ds(k * m + up, m - up)]

    def over(i):
        send(x_rest(i), x_rest(i), xs, vyr.at[lax.rem(order[i], NX)], ypair)

    def back(i):
        arrived(x_rest(i), vyr.at[lax.rem(order[i], NX)])

    def hand(i):
        send(half(order[i]), half(order[i]), cs, cr.at[order[i]], core)

    def quarter(p):
        return pl.ds(pl.multiple_of(p * q, q), q)

    def with_quarter(p, do):
        @pl.when(p < NY - 1)
        def _():
            do(quarter(p), q)

        @pl.when(p == NY - 1)
        def _():
            do(pl.ds((NY - 1) * q, ql), ql)

    def spread(src, dst, ss, rs):
        for d in (1, 3, 2):
            with_quarter(at_y(d), lambda rows, n: send(src.at[rows], dst.at[yh, pl.ds(0, n)], ss, rs, ydev[d]))

    def quarters_in(buf, rs):
        with_quarter(yh, lambda rows, n: arrived(buf.at[pl.ds(0, NY - 1), pl.ds(0, n)], rs))

    def to_owner(i, src, dst, ss, rs):
        to = owner(order[i])

        @pl.when(to != z)
        def _():
            send(src, dst.at[z], ss, rs, (rid(z=to), c))

        @pl.when(to == z)
        def _():
            dst[z] = src[...]

    def add_up(buf, out):
        value = buf[0].astype(F32)
        for s in range(1, buf.shape[0]):
            value = value + buf[s].astype(F32)
        out[...] = value.astype(out.dtype)

    def partial(i):
        b = order[i]
        if i:
            arrived(other(b), cr.at[b])
        sb[i] = jnp.dot(lt[...], xx[b], preferred_element_type=F32).astype(BF16)
        if i < EARLY:
            to_owner(i, sb.at[i], rb, zs, zr)
        else:
            j = i - EARLY
            yb[j, yh] = sb[i, quarter(yh)]
            spread(sb.at[i], yb.at[j], ys, yr.at[j])

    def late(i):
        j = i - EARLY
        quarters_in(yb.at[j], yr.at[j])
        add_up(yb.at[j], qb.at[j])
        to_owner(i, qb.at[j], zb, zqs, zqr)

    rring = (x_half, xs, lambda b, n: xr.at[lax.rem(b, NX), n], xdev, xslots)
    rring2 = (x_quarter, xs, lambda b, n: xr2.at[lax.rem(b, NX), n], xdev, xslots2)
    send(half(c), half(c), xs, wr, ypair)
    ring_step(*rring, 0)
    hand(0)
    pick = (
        lax.broadcasted_iota(jnp.int32, (hp, w), 1) == lax.broadcasted_iota(jnp.int32, (hp, w), 0) + k * h
    ).astype(BF16)
    arrived(other(c), cr.at[c])
    lt[...] = lax.dot_general(
        pick, xx[c], (((1,), (1,)), ((), ())), preferred_element_type=F32
    ).astype(BF16)
    partial(0)
    ring_step(*rring, 1)
    over(2)
    over(3)
    hand(2)
    hand(3)
    arrived(half(c2), wr)
    ring_step(*rring2, 0)
    hand(1)
    partial(2)
    partial(3)
    partial(1)
    ring_step(*rring, 2)
    over(4)
    hand(4)
    ring_step(*rring2, 1)
    for i in (5, 6):
        back(i)
        hand(i)
    partial(4)
    partial(5)
    partial(6)
    ring_step(*rring2, 2)
    back(7)
    hand(7)
    partial(7)
    mine_early = owner(order[0]) == z
    for i in range(1, EARLY):
        mine_early = jnp.logical_or(mine_early, owner(order[i]) == z)

    def start_early():
        @pl.when(mine_early)
        def _():
            arrived(rb.at[pl.ds(0, NZ - 1)], zr)
            add_up(rb, eb)
            yb[NB - EARLY, yh] = eb[quarter(yh)]
            spread(eb, yb.at[NB - EARLY], es, yr.at[NB - EARLY])

    for i in range(EARLY, NB):
        if i == POS:
            start_early()
        late(i)
    if POS == NB:
        start_early()

    @pl.when(mine_early)
    def _():
        quarters_in(yb.at[NB - EARLY], yr.at[NB - EARLY])
        add_up(yb.at[NB - EARLY], tot)

    @pl.when(jnp.logical_not(mine_early))
    def _():
        arrived(zb.at[pl.ds(0, NZ - 1)], zqr)
        add_up(zb, tot)

    top = pl.ds(k * h, h)
    low = pl.ds((1 - k) * h, h)
    columns = [ypair] + [xdev[d] for d in (1, 3, 2)] + [(r, xslots2[d]) for d in (1, 3, 2)]

    def over_z(s, rows, j, hop, right):
        if hop < NZ // 2 - (right == j % 2):
            g = gl.at[s, rows]
            send(g, g, gzs, gzr.at[s, j], zdev[1 if right else -1])

    def set_off(j):
        def go(rows, n):
            g = gl.at[z, rows]
            if j == 0:
                gl[z, rows] = (tot[pl.ds(0, n)] / ROWS).astype(BF16)
                for d in (1, 3, 2):
                    send(g, g, as_, ar.at[NY - d], ydev[d])
            else:
                arrived(g, ar.at[j])
            for right in (1, 0):
                over_z(z, rows, j, 0, right)
            for to in columns:
                send(g, gr.at[c, pl.ds(pl.multiple_of(k * h + rows.start, 16), n)], gxs, gxr.at[c], to)

        with_quarter(at_y(j), go)

    def hops(step, js):
        for j in js:
            for right in (1, 0):
                if step <= NZ // 2 - (right == j % 2):
                    s = zslots[-step if right else step]

                    def go(rows, n):
                        arrived(gl.at[s, rows], gzr.at[s, j])
                        over_z(s, rows, j, step, right)

                    with_quarter(at_y(j), go)

    def hand_on(slots):
        for b in slots:
            send(gr.at[b, top], gr.at[b, top], gcs, gcr, core)

    def columns_in(slots):
        for b in slots:
            arrived(gr.at[b, top], gxr.at[b])
            hand_on([b])

    set_off(0)
    set_off(1)
    set_off(3)
    hops(1, (0,))
    set_off(2)
    gram = gl[z]
    gr[c, top, :] = gram
    hand_on([c])
    hops(1, (1, 3))
    hops(2, (0,))
    hops(1, (2,))
    hops(2, (1, 3))
    hops(3, (0,))
    hops(2, (2,))
    columns_in(order[1:4])
    hops(3, (1, 3))
    hops(3, (2,))
    columns_in(order[4:])
    def square_term(s):
        return jnp.dot(gl[s], gr[block(s)], preferred_element_type=F32)

    arrived(gr.at[:, pl.ds(0, h)], gcr)
    square = square_term(z)
    for d in (1, 7, 2, 6, 3, 5):
        square = square + square_term(zslots[d])
    hops(4, (0, 1, 3, 2))
    square = square + square_term(zslots[4])
    pf[z, top, :] = (coef_b * gram.astype(F32) + coef_c * square).astype(BF16)
    def p_row(s, n):
        return pf.at[s, pl.ds(k * h + n * cut, h - cut if n else cut)]

    pring = (p_row, pzs, lambda s, n: pzr.at[s, n], zdev, zslots)

    def hand_over(slots):
        for s in slots:
            send(pf.at[s, top], pf.at[s, top], pcs, pcr.at[s], core)

    def term(s):
        arrived(pf.at[s, low], pcr.at[s])
        return lax.dot_general(
            xx[block(s), pl.ds(k * m, m)], pf[s], (((1,), (1,)), ((), ())), preferred_element_type=F32
        )

    ring_step(*pring, 0)
    hand_over([z])
    update = None
    held = [z]
    for step in range(1, 5):
        ring_step(*pring, step)
        got = [zslots[-step], zslots[step]] if step < 4 else [zslots[4]]
        hand_over(got)
        for s in held:
            update = term(s) if update is None else update + term(s)
        held = got
    for s in held:
        update = update + term(s)
    o_ref[...] = (coef_a * xx[c, pl.ds(k * m, m)].astype(F32) + update).astype(BF16)

    sent(xx.at[pl.ds(0, NB - 1), pl.ds(0, m)], xs)
    sent(xx.at[:, pl.ds(0, m)], cs)

    @pl.when(mine_early)
    def _():
        sent(sb.at[pl.ds(0, EARLY - 1)], zs)
        sent(qb, zqs)
        with_quarter(yh, lambda rows, n: sent(eb.at[pl.ds(0, h - n)], es))

    @pl.when(jnp.logical_not(mine_early))
    def _():
        sent(sb.at[pl.ds(0, EARLY)], zs)
        sent(qb.at[pl.ds(0, NB - EARLY - 1)], zqs)

    with_quarter(yh, lambda rows, n: sent(sb.at[pl.ds(0, NB - EARLY), pl.ds(0, h - n)], ys))
    with_quarter(yh, lambda rows, n: sent(gl.at[pl.ds(0, NY - 1), pl.ds(0, n)], as_))
    sent(gl.at[pl.ds(0, NZ - 1)], gzs)
    sent(gr.at[pl.ds(0, NB - 1), pl.ds(0, h)], gxs)
    sent(gr.at[:, pl.ds(0, h)], gcs)
    sent(pf.at[pl.ds(0, NZ - 1), pl.ds(0, h)], pzs)
    sent(pf.at[:, pl.ds(0, h)], pcs)


def local(momentum):
    m, w = momentum.shape
    h = w // 2
    q = -(-h // (16 * NY)) * 16
    dma = lambda *n: pltpu.SemaphoreType.DMA(n)
    one = pltpu.SemaphoreType.DMA
    return pl.pallas_call(
        kernel,
        out_shape=jax.ShapeDtypeStruct((m, w), BF16),
        in_specs=[pl.BlockSpec(memory_space=pl.ANY)],
        out_specs=pl.BlockSpec(memory_space=pltpu.VMEM),
        scratch_shapes=[
            pltpu.VMEM((NB, 2 * m, w), BF16),
            pltpu.VMEM((NB, NY * q, w), BF16),
            pltpu.VMEM((NZ, NY * q, w), BF16),
            pltpu.VMEM((NY * q, w), BF16),
            pltpu.VMEM((NB - EARLY + 1, NY, q, w), BF16),
            pltpu.VMEM((NB - EARLY, q, w), BF16),
            pltpu.VMEM((NZ, q, w), BF16),
            pltpu.VMEM((q, w), F32),
            pltpu.VMEM((NZ, h, w), BF16),
            pltpu.VMEM((NB, w, w), BF16),
            pltpu.VMEM((NZ, w, w), BF16),
            pltpu.VMEM((NY * q, 2 * m), BF16),
            one, one, one, one, one, one, one, one, one, one, one, one, one,
            one, dma(NX, 2), dma(NX, 2), dma(NX), dma(NB), one, one, dma(NB - EARLY + 1), dma(NY),
            dma(NZ, NY), dma(NB), one, dma(NZ, 2), dma(NZ),
        ],
        compiler_params=pltpu.CompilerParams(
            collective_id=0, has_side_effects=True, vmem_limit_bytes=48 << 20
        ),
        name="newton_schulz",
    )(momentum)


def solution(mesh):
    return jax.shard_map(
        local,
        mesh=mesh,
        in_specs=(P("rows", "cols"),),
        out_specs=P("rows", "cols"),
        check_vma=False,
    )
```

```python
import jax
import jax.numpy as jnp
from jax import lax
from jax.experimental import pallas as pl
from jax.experimental.pallas import tpu as pltpu
from jax.sharding import PartitionSpec as P

ROWS = 25600

coef_a = 3.4445
coef_b = -4.775
coef_c = 2.0315

NZ, NY, NX = 8, 4, 4
NB = 8
EARLY = 4
UP = 256
START = 7
MESH = pl.DeviceIdType.MESH
F32, BF16 = jnp.float32, jnp.bfloat16


def kernel(
    x_hbm, o_ref, xx, sb, rb, eb, yb, qb, zb, tot, gl, gr, pf, lt,
    loc, xs, cs, zs, zqs, ys, es, as_, gzs, gxs, gcs, pzs, pcs,
    wr, xr, xr2, vyr, cr, zr, zqr, yr, ar, gzr, gxr, gcr, pzr, pcr,
):
    m, w = x_hbm.shape
    h = w // 2
    q = qb.shape[1]
    hp = NY * q
    ql = h - (NY - 1) * q
    cut = -(-h // 32) * 16
    mid = -(-m // 32) * 16
    up = UP
    qtr = -(-up // 32) * 16
    r, c = lax.axis_index("rows"), lax.axis_index("cols")
    z, yh, k = r // (NY * 2), lax.rem(r // 2, NY), lax.rem(r, 2)
    yl, x = c // NX, lax.rem(c, NX)

    def rid(z=z, yh=yh, k=k):
        return (z * NY + yh) * 2 + k

    def cid(yl=yl, x=x):
        return yl * NX + x

    def at_x(d):
        return lax.rem(x + d, NX)

    def at_z(d):
        return lax.rem(z + d, NZ)

    def at_y(d):
        return lax.rem(yh + d, NY)

    core = (rid(k=1 - k), c)
    ypair = (r, cid(yl=1 - yl))
    xdev = [(r, cid(x=at_x(d))) for d in range(NX)]
    zdev = [(rid(z=at_z(d)), c) for d in range(NZ)]
    ydev = [(rid(yh=at_y(d)), c) for d in range(NY)]

    def copy(src, dst, ss, rs, to):
        return pltpu.make_async_remote_copy(
            src_ref=src, dst_ref=dst, send_sem=ss, recv_sem=rs, device_id=to, device_id_type=MESH
        )

    def send(src, dst, ss, rs, to):
        copy(src, dst, ss, rs, to).start()

    def arrived(dst, rs):
        copy(dst, dst, loc, rs, core).wait_recv()

    def sent(src, ss):
        copy(src, src, ss, loc, core).wait_send()

    mine = xx.at[c, pl.ds(k * m, m)]
    own = pltpu.make_async_copy(x_hbm, mine, loc)
    own.start()
    barrier = pltpu.get_barrier_semaphore()
    partners = [core, ypair] + xdev[1:] + [(r, cid(yl=1 - yl, x=at_x(d))) for d in (1, 2, 3)] + zdev[1:] + ydev[1:]
    for to in partners:
        pl.semaphore_signal(barrier, inc=1, device_id=to, device_id_type=MESH)
    pl.semaphore_wait(barrier, len(partners))
    own.wait()

    xslots = [cid(x=at_x(d)) for d in range(NX)]
    xslots2 = [cid(yl=1 - yl, x=at_x(d)) for d in range(NX)]
    zslots = [at_z(d) for d in range(NZ)]
    order = [xslots[0], xslots2[0]] + [xslots[d] for d in (1, 3, 2)] + [xslots2[d] for d in (1, 3, 2)]
    c2 = order[1]

    def owner(b):
        return lax.rem(b, NX) * 2 + b // NX

    def block(s):
        return s % 2 * NX + s // 2 if isinstance(s, int) else lax.rem(s, 2) * NX + s // 2

    def ring_hop(buf, ss, rs, dev, slots, hop, right, n):
        reach = len(slots) // 2 - (right == n % 2)
        if hop > reach:
            return
        s = slots[-hop if right else hop] if hop else slots[0]
        if hop:
            arrived(buf(s, n), rs(s, n))
        if hop < reach:
            send(buf(s, n), buf(s, n), ss, rs(s, n), dev[1 if right else -1])

    def ring_step(*args):
        for right, n in ((1, 0), (0, 1), (1, 1), (0, 0)):
            ring_hop(*args, right, n)

    def half(b):
        return xx.at[b, pl.ds(k * m, m)]

    def other(b):
        return xx.at[b, pl.ds((1 - k) * m, m)]

    def x_half(b, n):
        return xx.at[b, pl.ds(k * m + n * mid, m - mid if n else mid)]

    def x_quarter(b, n):
        return xx.at[b, pl.ds(k * m + n * qtr, up - qtr if n else qtr)]

    def x_rest(i):
        return xx.at[order[i], pl.ds(k * m + up, m - up)]

    def over(i):
        send(x_rest(i), x_rest(i), xs, vyr.at[lax.rem(order[i], NX)], ypair)

    def back(i):
        arrived(x_rest(i), vyr.at[lax.rem(order[i], NX)])

    def hand(i):
        send(half(order[i]), half(order[i]), cs, cr.at[order[i]], core)

    def quarter(p):
        return pl.ds(pl.multiple_of(p * q, q), q)

    def with_quarter(p, do):
        @pl.when(p < NY - 1)
        def _():
            do(quarter(p), q)

        @pl.when(p == NY - 1)
        def _():
            do(pl.ds((NY - 1) * q, ql), ql)

    def spread(src, dst, ss, rs):
        for d in (1, 3, 2):
            with_quarter(at_y(d), lambda rows, n: send(src.at[rows], dst.at[yh, pl.ds(0, n)], ss, rs, ydev[d]))

    def quarters_in(buf, rs):
        with_quarter(yh, lambda rows, n: arrived(buf.at[pl.ds(0, NY - 1), pl.ds(0, n)], rs))

    def to_owner(i, src, dst, ss, rs):
        to = owner(order[i])

        @pl.when(to != z)
        def _():
            send(src, dst.at[z], ss, rs, (rid(z=to), c))

        @pl.when(to == z)
        def _():
            dst[z] = src[...]

    def add_up(buf, out):
        value = buf[0].astype(F32)
        for s in range(1, buf.shape[0]):
            value = value + buf[s].astype(F32)
        out[...] = value.astype(out.dtype)

    def partial(i):
        b = order[i]
        if i:
            arrived(other(b), cr.at[b])
        sb[i] = jnp.dot(lt[...], xx[b], preferred_element_type=F32).astype(BF16)
        if i < EARLY:
            to_owner(i, sb.at[i], rb, zs, zr)
        else:
            j = i - EARLY
            yb[j, yh] = sb[i, quarter(yh)]
            spread(sb.at[i], yb.at[j], ys, yr.at[j])

    def late(i):
        j = i - EARLY
        quarters_in(yb.at[j], yr.at[j])
        add_up(yb.at[j], qb.at[j])
        to_owner(i, qb.at[j], zb, zqs, zqr)

    rring = (x_half, xs, lambda b, n: xr.at[lax.rem(b, NX), n], xdev, xslots)
    rring2 = (x_quarter, xs, lambda b, n: xr2.at[lax.rem(b, NX), n], xdev, xslots2)
    send(half(c), half(c), xs, wr, ypair)
    ring_step(*rring, 0)
    hand(0)
    pick = (
        lax.broadcasted_iota(jnp.int32, (hp, w), 1) == lax.broadcasted_iota(jnp.int32, (hp, w), 0) + k * h
    ).astype(BF16)
    arrived(other(c), cr.at[c])
    lt[...] = lax.dot_general(
        pick, xx[c], (((1,), (1,)), ((), ())), preferred_element_type=F32
    ).astype(BF16)
    partial(0)
    ring_step(*rring, 1)
    over(2)
    over(3)
    hand(2)
    hand(3)
    arrived(half(c2), wr)
    ring_step(*rring2, 0)
    hand(1)
    partial(2)
    partial(3)
    partial(1)
    ring_step(*rring, 2)
    over(4)
    hand(4)
    ring_step(*rring2, 1)
    for i in (5, 6):
        back(i)
        hand(i)
    partial(4)
    partial(5)
    partial(6)
    ring_step(*rring2, 2)
    back(7)
    hand(7)
    partial(7)
    mine_early = owner(order[0]) == z
    for i in range(1, EARLY):
        mine_early = jnp.logical_or(mine_early, owner(order[i]) == z)

    def start_early():
        @pl.when(mine_early)
        def _():
            arrived(rb.at[pl.ds(0, NZ - 1)], zr)
            add_up(rb, eb)
            yb[NB - EARLY, yh] = eb[quarter(yh)]
            spread(eb, yb.at[NB - EARLY], es, yr.at[NB - EARLY])

    for i in range(EARLY, NB):
        if i == START:
            start_early()
        late(i)
    if START == NB:
        start_early()

    @pl.when(mine_early)
    def _():
        quarters_in(yb.at[NB - EARLY], yr.at[NB - EARLY])
        add_up(yb.at[NB - EARLY], tot)

    @pl.when(jnp.logical_not(mine_early))
    def _():
        arrived(zb.at[pl.ds(0, NZ - 1)], zqr)
        add_up(zb, tot)

    top = pl.ds(k * h, h)
    low = pl.ds((1 - k) * h, h)
    columns = [ypair] + [xdev[d] for d in (1, 3, 2)] + [(r, xslots2[d]) for d in (1, 3, 2)]

    def over_z(s, rows, j, hop, right):
        if hop < NZ // 2 - (right == j % 2):
            g = gl.at[s, rows]
            send(g, g, gzs, gzr.at[s, j], zdev[1 if right else -1])

    def set_off(j):
        def go(rows, n):
            g = gl.at[z, rows]
            if j == 0:
                gl[z, rows] = (tot[pl.ds(0, n)] / ROWS).astype(BF16)
                for d in (1, 3, 2):
                    send(g, g, as_, ar.at[NY - d], ydev[d])
            else:
                arrived(g, ar.at[j])
            for right in (1, 0):
                over_z(z, rows, j, 0, right)
            for to in columns:
                send(g, gr.at[c, pl.ds(pl.multiple_of(k * h + rows.start, 16), n)], gxs, gxr.at[c], to)

        with_quarter(at_y(j), go)

    def hops(step, js):
        for j in js:
            for right in (1, 0):
                if step <= NZ // 2 - (right == j % 2):
                    s = zslots[-step if right else step]

                    def go(rows, n):
                        arrived(gl.at[s, rows], gzr.at[s, j])
                        over_z(s, rows, j, step, right)

                    with_quarter(at_y(j), go)

    def hand_on(slots):
        for b in slots:
            send(gr.at[b, top], gr.at[b, top], gcs, gcr, core)

    def columns_in(slots):
        for b in slots:
            arrived(gr.at[b, top], gxr.at[b])
            hand_on([b])

    set_off(0)
    set_off(1)
    set_off(3)
    hops(1, (0,))
    set_off(2)
    gram = gl[z]
    gr[c, top, :] = gram
    hand_on([c])
    hops(1, (1, 3))
    hops(2, (0,))
    hops(1, (2,))
    hops(2, (1, 3))
    hops(3, (0,))
    hops(2, (2,))
    columns_in(order[1:4])
    hops(3, (1, 3))
    hops(3, (2,))
    columns_in(order[4:])
    def square_term(s):
        return jnp.dot(gl[s], gr[block(s)], preferred_element_type=F32)

    arrived(gr.at[:, pl.ds(0, h)], gcr)
    square = square_term(z)
    for d in (1, 7, 2, 6, 3, 5):
        square = square + square_term(zslots[d])
    hops(4, (0, 1, 3, 2))
    square = square + square_term(zslots[4])
    pf[z, top, :] = (coef_b * gram.astype(F32) + coef_c * square).astype(BF16)
    def p_row(s, n):
        return pf.at[s, pl.ds(k * h + n * q, min(q, h - n * q))]

    def ring_step4(*args):
        for right, n in ((1, 0), (0, 1), (1, 2), (0, 3), (1, 1), (0, 0), (1, 3), (0, 2)):
            ring_hop(*args, right, n)

    pring = (p_row, pzs, lambda s, n: pzr.at[s, n], zdev, zslots)

    def hand_over(slots):
        for s in slots:
            send(pf.at[s, top], pf.at[s, top], pcs, pcr.at[s], core)

    def term(s):
        arrived(pf.at[s, low], pcr.at[s])
        return lax.dot_general(
            xx[block(s), pl.ds(k * m, m)], pf[s], (((1,), (1,)), ((), ())), preferred_element_type=F32
        )

    ring_step4(*pring, 0)
    hand_over([z])
    update = None
    held = [z]
    for step in range(1, 5):
        ring_step4(*pring, step)
        got = [zslots[-step], zslots[step]] if step < 4 else [zslots[4]]
        hand_over(got)
        for s in held:
            update = term(s) if update is None else update + term(s)
        held = got
    for s in held:
        update = update + term(s)
    o_ref[...] = (coef_a * xx[c, pl.ds(k * m, m)].astype(F32) + update).astype(BF16)

    sent(xx.at[pl.ds(0, NB - 1), pl.ds(0, m)], xs)
    sent(xx.at[:, pl.ds(0, m)], cs)

    @pl.when(mine_early)
    def _():
        sent(sb.at[pl.ds(0, EARLY - 1)], zs)
        sent(qb, zqs)
        with_quarter(yh, lambda rows, n: sent(eb.at[pl.ds(0, h - n)], es))

    @pl.when(jnp.logical_not(mine_early))
    def _():
        sent(sb.at[pl.ds(0, EARLY)], zs)
        sent(qb.at[pl.ds(0, NB - EARLY - 1)], zqs)

    with_quarter(yh, lambda rows, n: sent(sb.at[pl.ds(0, NB - EARLY), pl.ds(0, h - n)], ys))
    with_quarter(yh, lambda rows, n: sent(gl.at[pl.ds(0, NY - 1), pl.ds(0, n)], as_))
    sent(gl.at[pl.ds(0, NZ - 1)], gzs)
    sent(gr.at[pl.ds(0, NB - 1), pl.ds(0, h)], gxs)
    sent(gr.at[:, pl.ds(0, h)], gcs)
    sent(pf.at[pl.ds(0, NZ - 1), pl.ds(0, h)], pzs)
    sent(pf.at[:, pl.ds(0, h)], pcs)


def local(momentum):
    m, w = momentum.shape
    h = w // 2
    q = -(-h // (16 * NY)) * 16
    dma = lambda *n: pltpu.SemaphoreType.DMA(n)
    one = pltpu.SemaphoreType.DMA
    return pl.pallas_call(
        kernel,
        out_shape=jax.ShapeDtypeStruct((m, w), BF16),
        in_specs=[pl.BlockSpec(memory_space=pl.ANY)],
        out_specs=pl.BlockSpec(memory_space=pltpu.VMEM),
        scratch_shapes=[
            pltpu.VMEM((NB, 2 * m, w), BF16),
            pltpu.VMEM((NB, NY * q, w), BF16),
            pltpu.VMEM((NZ, NY * q, w), BF16),
            pltpu.VMEM((NY * q, w), BF16),
            pltpu.VMEM((NB - EARLY + 1, NY, q, w), BF16),
            pltpu.VMEM((NB - EARLY, q, w), BF16),
            pltpu.VMEM((NZ, q, w), BF16),
            pltpu.VMEM((q, w), F32),
            pltpu.VMEM((NZ, h, w), BF16),
            pltpu.VMEM((NB, w, w), BF16),
            pltpu.VMEM((NZ, w, w), BF16),
            pltpu.VMEM((NY * q, 2 * m), BF16),
            one, one, one, one, one, one, one, one, one, one, one, one, one,
            one, dma(NX, 2), dma(NX, 2), dma(NX), dma(NB), one, one, dma(NB - EARLY + 1), dma(NY),
            dma(NZ, NY), dma(NB), one, dma(NZ, NY), dma(NZ),
        ],
        compiler_params=pltpu.CompilerParams(
            collective_id=0, has_side_effects=True, vmem_limit_bytes=48 << 20
        ),
        name="newton_schulz",
    )(momentum)


def solution(mesh):
    return jax.shard_map(
        local,
        mesh=mesh,
        in_specs=(P("rows", "cols"),),
        out_specs=P("rows", "cols"),
        check_vma=False,
    )
```

```python
import jax
import jax.numpy as jnp
from jax import lax
from jax.experimental import pallas as pl
from jax.experimental.pallas import tpu as pltpu
from jax.sharding import PartitionSpec as P

ROWS = 25600

coef_a = 3.4445
coef_b = -4.775
coef_c = 2.0315

NZ, NY, NX = 8, 4, 4
NB = 8
EARLY = 4
UP = 256
START = 7
MESH = pl.DeviceIdType.MESH
F32, BF16 = jnp.float32, jnp.bfloat16


def kernel(
    x_hbm, o_ref, xx, sb, rb, eb, yb, qb, zb, tot, gl, gr, pf, lt,
    loc, xs, cs, zs, zqs, ys, es, as_, gzs, gxs, gcs, pzs, pcs,
    wr, xr, xr2, vyr, cr, zr, zqr, yr, ar, gzr, gxr, gcr, pzr, pcr,
):
    m, w = x_hbm.shape
    h = w // 2
    q = qb.shape[1]
    hp = NY * q
    ql = h - (NY - 1) * q
    cut = -(-h // 32) * 16
    mid = -(-m // 32) * 16
    up = UP
    qtr = -(-up // 32) * 16
    r, c = lax.axis_index("rows"), lax.axis_index("cols")
    z, yh, k = r // (NY * 2), lax.rem(r // 2, NY), lax.rem(r, 2)
    yl, x = c // NX, lax.rem(c, NX)

    def rid(z=z, yh=yh, k=k):
        return (z * NY + yh) * 2 + k

    def cid(yl=yl, x=x):
        return yl * NX + x

    def at_x(d):
        return lax.rem(x + d, NX)

    def at_z(d):
        return lax.rem(z + d, NZ)

    def at_y(d):
        return lax.rem(yh + d, NY)

    core = (rid(k=1 - k), c)
    ypair = (r, cid(yl=1 - yl))
    xdev = [(r, cid(x=at_x(d))) for d in range(NX)]
    zdev = [(rid(z=at_z(d)), c) for d in range(NZ)]
    ydev = [(rid(yh=at_y(d)), c) for d in range(NY)]

    def copy(src, dst, ss, rs, to):
        return pltpu.make_async_remote_copy(
            src_ref=src, dst_ref=dst, send_sem=ss, recv_sem=rs, device_id=to, device_id_type=MESH
        )

    def send(src, dst, ss, rs, to):
        copy(src, dst, ss, rs, to).start()

    def arrived(dst, rs):
        copy(dst, dst, loc, rs, core).wait_recv()

    def sent(src, ss):
        copy(src, src, ss, loc, core).wait_send()

    mine = xx.at[c, pl.ds(k * m, m)]
    own = pltpu.make_async_copy(x_hbm, mine, loc)
    own.start()
    barrier = pltpu.get_barrier_semaphore()
    partners = [core, ypair] + xdev[1:] + [(r, cid(yl=1 - yl, x=at_x(d))) for d in (1, 2, 3)] + zdev[1:] + ydev[1:]
    for to in partners:
        pl.semaphore_signal(barrier, inc=1, device_id=to, device_id_type=MESH)
    pl.semaphore_wait(barrier, len(partners))
    own.wait()

    xslots = [cid(x=at_x(d)) for d in range(NX)]
    xslots2 = [cid(yl=1 - yl, x=at_x(d)) for d in range(NX)]
    zslots = [at_z(d) for d in range(NZ)]
    order = [xslots[0], xslots2[0]] + [xslots[d] for d in (1, 3, 2)] + [xslots2[d] for d in (1, 3, 2)]
    c2 = order[1]

    def owner(b):
        return lax.rem(b, NX) * 2 + b // NX

    def block(s):
        return s % 2 * NX + s // 2 if isinstance(s, int) else lax.rem(s, 2) * NX + s // 2

    def ring_hop(buf, ss, rs, dev, slots, hop, right, n):
        reach = len(slots) // 2 - (right == n % 2)
        if hop > reach:
            return
        s = slots[-hop if right else hop] if hop else slots[0]
        if hop:
            arrived(buf(s, n), rs(s, n))
        if hop < reach:
            send(buf(s, n), buf(s, n), ss, rs(s, n), dev[1 if right else -1])

    def ring_step(*args):
        for right, n in ((1, 0), (0, 1), (1, 1), (0, 0)):
            ring_hop(*args, right, n)

    def half(b):
        return xx.at[b, pl.ds(k * m, m)]

    def other(b):
        return xx.at[b, pl.ds((1 - k) * m, m)]

    def x_half(b, n):
        return xx.at[b, pl.ds(k * m + n * mid, m - mid if n else mid)]

    def x_quarter(b, n):
        return xx.at[b, pl.ds(k * m + n * qtr, up - qtr if n else qtr)]

    def x_rest(i):
        return xx.at[order[i], pl.ds(k * m + up, m - up)]

    def over(i):
        send(x_rest(i), x_rest(i), xs, vyr.at[lax.rem(order[i], NX)], ypair)

    def back(i):
        arrived(x_rest(i), vyr.at[lax.rem(order[i], NX)])

    def hand(i):
        send(half(order[i]), half(order[i]), cs, cr.at[order[i]], core)

    def quarter(p):
        return pl.ds(pl.multiple_of(p * q, q), q)

    def with_quarter(p, do):
        @pl.when(p < NY - 1)
        def _():
            do(quarter(p), q)

        @pl.when(p == NY - 1)
        def _():
            do(pl.ds((NY - 1) * q, ql), ql)

    def spread(src, dst, ss, rs):
        for d in (1, 3, 2):
            with_quarter(at_y(d), lambda rows, n: send(src.at[rows], dst.at[yh, pl.ds(0, n)], ss, rs, ydev[d]))

    def quarters_in(buf, rs):
        with_quarter(yh, lambda rows, n: arrived(buf.at[pl.ds(0, NY - 1), pl.ds(0, n)], rs))

    def to_owner(i, src, dst, ss, rs):
        to = owner(order[i])

        @pl.when(to != z)
        def _():
            send(src, dst.at[z], ss, rs, (rid(z=to), c))

        @pl.when(to == z)
        def _():
            dst[z] = src[...]

    def add_up(buf, out):
        value = buf[0].astype(F32)
        for s in range(1, buf.shape[0]):
            value = value + buf[s].astype(F32)
        out[...] = value.astype(out.dtype)

    def partial(i):
        b = order[i]
        if i:
            arrived(other(b), cr.at[b])
        sb[i] = jnp.dot(lt[...], xx[b], preferred_element_type=F32).astype(BF16)
        if i < EARLY:
            to_owner(i, sb.at[i], rb, zs, zr)
        else:
            j = i - EARLY
            yb[j, yh] = sb[i, quarter(yh)]
            spread(sb.at[i], yb.at[j], ys, yr.at[j])

    def late(i):
        j = i - EARLY
        quarters_in(yb.at[j], yr.at[j])
        add_up(yb.at[j], qb.at[j])
        to_owner(i, qb.at[j], zb, zqs, zqr)

    rring = (x_half, xs, lambda b, n: xr.at[lax.rem(b, NX), n], xdev, xslots)
    rring2 = (x_quarter, xs, lambda b, n: xr2.at[lax.rem(b, NX), n], xdev, xslots2)
    send(half(c), half(c), xs, wr, ypair)
    ring_step(*rring, 0)
    hand(0)
    pick = (
        lax.broadcasted_iota(jnp.int32, (hp, w), 1) == lax.broadcasted_iota(jnp.int32, (hp, w), 0) + k * h
    ).astype(BF16)
    arrived(other(c), cr.at[c])
    lt[...] = lax.dot_general(
        pick, xx[c], (((1,), (1,)), ((), ())), preferred_element_type=F32
    ).astype(BF16)
    partial(0)
    ring_step(*rring, 1)
    over(2)
    over(3)
    hand(2)
    hand(3)
    arrived(half(c2), wr)
    ring_step(*rring2, 0)
    hand(1)
    partial(2)
    partial(3)
    partial(1)
    ring_step(*rring, 2)
    over(4)
    hand(4)
    ring_step(*rring2, 1)
    for i in (5, 6):
        back(i)
        hand(i)
    partial(4)
    partial(5)
    partial(6)
    ring_step(*rring2, 2)
    back(7)
    hand(7)
    partial(7)
    mine_early = owner(order[0]) == z
    for i in range(1, EARLY):
        mine_early = jnp.logical_or(mine_early, owner(order[i]) == z)

    def start_early():
        @pl.when(mine_early)
        def _():
            arrived(rb.at[pl.ds(0, NZ - 1)], zr)
            add_up(rb, eb)
            yb[NB - EARLY, yh] = eb[quarter(yh)]
            spread(eb, yb.at[NB - EARLY], es, yr.at[NB - EARLY])

    for i in range(EARLY, NB):
        if i == START:
            start_early()
        late(i)
    if START == NB:
        start_early()

    @pl.when(mine_early)
    def _():
        quarters_in(yb.at[NB - EARLY], yr.at[NB - EARLY])
        add_up(yb.at[NB - EARLY], tot)

    @pl.when(jnp.logical_not(mine_early))
    def _():
        arrived(zb.at[pl.ds(0, NZ - 1)], zqr)
        add_up(zb, tot)

    top = pl.ds(k * h, h)
    low = pl.ds((1 - k) * h, h)
    columns = [ypair] + [xdev[d] for d in (1, 3, 2)] + [(r, xslots2[d]) for d in (1, 3, 2)]

    def over_z(s, rows, j, hop, right):
        if hop < NZ // 2 - (right == j % 2):
            g = gl.at[s, rows]
            send(g, g, gzs, gzr.at[s, j], zdev[1 if right else -1])

    def set_off(j):
        def go(rows, n):
            g = gl.at[z, rows]
            if j == 0:
                gl[z, rows] = (tot[pl.ds(0, n)] / ROWS).astype(BF16)
                for d in (1, 3, 2):
                    send(g, g, as_, ar.at[NY - d], ydev[d])
            else:
                arrived(g, ar.at[j])
            for right in (1, 0):
                over_z(z, rows, j, 0, right)
            for to in columns:
                send(g, gr.at[c, pl.ds(pl.multiple_of(k * h + rows.start, 16), n)], gxs, gxr.at[c], to)

        with_quarter(at_y(j), go)

    def hops(step, js):
        for j in js:
            for right in (1, 0):
                if step <= NZ // 2 - (right == j % 2):
                    s = zslots[-step if right else step]

                    def go(rows, n):
                        arrived(gl.at[s, rows], gzr.at[s, j])
                        over_z(s, rows, j, step, right)

                    with_quarter(at_y(j), go)

    def hand_on(slots):
        for b in slots:
            send(gr.at[b, top], gr.at[b, top], gcs, gcr, core)

    def columns_in(slots):
        for b in slots:
            arrived(gr.at[b, top], gxr.at[b])
            hand_on([b])

    set_off(0)
    set_off(1)
    set_off(3)
    hops(1, (0,))
    set_off(2)
    gram = gl[z]
    gr[c, top, :] = gram
    hand_on([c])
    hops(1, (1, 3))
    hops(2, (0,))
    hops(1, (2,))
    hops(2, (1, 3))
    hops(3, (0,))
    hops(2, (2,))
    columns_in(order[1:4])
    hops(3, (1, 3))
    hops(3, (2,))
    columns_in(order[4:])
    def square_term(s):
        return jnp.dot(gl[s], gr[block(s)], preferred_element_type=F32)

    arrived(gr.at[:, pl.ds(0, h)], gcr)
    square = square_term(z)
    for d in (1, 7, 2, 6, 3, 5):
        square = square + square_term(zslots[d])
    hops(4, (0, 1, 3, 2))
    square = square + square_term(zslots[4])
    pf[z, top, :] = (coef_b * gram.astype(F32) + coef_c * square).astype(BF16)
    def p_row(s, n):
        return pf.at[s, pl.ds(k * h + n * q, min(q, h - n * q))]

    def ring_step4(*args):
        for right, n in ((1, 0), (0, 1), (1, 2), (0, 3), (1, 1), (0, 0), (1, 3), (0, 2)):
            ring_hop(*args, right, n)

    pring = (p_row, pzs, lambda s, n: pzr.at[s, n], zdev, zslots)

    def hand_over(slots):
        for s in slots:
            send(pf.at[s, top], pf.at[s, top], pcs, pcr.at[s], core)

    def term(s):
        arrived(pf.at[s, low], pcr.at[s])
        return lax.dot_general(
            xx[block(s), pl.ds(k * m, m)], pf[s], (((1,), (1,)), ((), ())), preferred_element_type=F32
        )

    ring_step4(*pring, 0)
    hand_over([z])
    update = None
    held = [z]
    for step in range(1, 5):
        got = [zslots[-step], zslots[step]] if step < 4 else [zslots[4]]
        if step < 4:
            ring_step4(*pring, step)
            hand_over(got)
        else:
            for right, n in ((1, 0), (0, 1), (1, 2), (0, 3)):
                ring_hop(*pring, step, right, n)
                send(p_row(got[0], n), p_row(got[0], n), pcs, pcr.at[got[0]], core)
        for s in held:
            update = term(s) if update is None else update + term(s)
        held = got
    for s in held:
        update = update + term(s)
    o_ref[...] = (coef_a * xx[c, pl.ds(k * m, m)].astype(F32) + update).astype(BF16)

    sent(xx.at[pl.ds(0, NB - 1), pl.ds(0, m)], xs)
    sent(xx.at[:, pl.ds(0, m)], cs)

    @pl.when(mine_early)
    def _():
        sent(sb.at[pl.ds(0, EARLY - 1)], zs)
        sent(qb, zqs)
        with_quarter(yh, lambda rows, n: sent(eb.at[pl.ds(0, h - n)], es))

    @pl.when(jnp.logical_not(mine_early))
    def _():
        sent(sb.at[pl.ds(0, EARLY)], zs)
        sent(qb.at[pl.ds(0, NB - EARLY - 1)], zqs)

    with_quarter(yh, lambda rows, n: sent(sb.at[pl.ds(0, NB - EARLY), pl.ds(0, h - n)], ys))
    with_quarter(yh, lambda rows, n: sent(gl.at[pl.ds(0, NY - 1), pl.ds(0, n)], as_))
    sent(gl.at[pl.ds(0, NZ - 1)], gzs)
    sent(gr.at[pl.ds(0, NB - 1), pl.ds(0, h)], gxs)
    sent(gr.at[:, pl.ds(0, h)], gcs)
    sent(pf.at[pl.ds(0, NZ - 1), pl.ds(0, h)], pzs)
    sent(pf.at[:, pl.ds(0, h)], pcs)


def local(momentum):
    m, w = momentum.shape
    h = w // 2
    q = -(-h // (16 * NY)) * 16
    dma = lambda *n: pltpu.SemaphoreType.DMA(n)
    one = pltpu.SemaphoreType.DMA
    return pl.pallas_call(
        kernel,
        out_shape=jax.ShapeDtypeStruct((m, w), BF16),
        in_specs=[pl.BlockSpec(memory_space=pl.ANY)],
        out_specs=pl.BlockSpec(memory_space=pltpu.VMEM),
        scratch_shapes=[
            pltpu.VMEM((NB, 2 * m, w), BF16),
            pltpu.VMEM((NB, NY * q, w), BF16),
            pltpu.VMEM((NZ, NY * q, w), BF16),
            pltpu.VMEM((NY * q, w), BF16),
            pltpu.VMEM((NB - EARLY + 1, NY, q, w), BF16),
            pltpu.VMEM((NB - EARLY, q, w), BF16),
            pltpu.VMEM((NZ, q, w), BF16),
            pltpu.VMEM((q, w), F32),
            pltpu.VMEM((NZ, h, w), BF16),
            pltpu.VMEM((NB, w, w), BF16),
            pltpu.VMEM((NZ, w, w), BF16),
            pltpu.VMEM((NY * q, 2 * m), BF16),
            one, one, one, one, one, one, one, one, one, one, one, one, one,
            one, dma(NX, 2), dma(NX, 2), dma(NX), dma(NB), one, one, dma(NB - EARLY + 1), dma(NY),
            dma(NZ, NY), dma(NB), one, dma(NZ, NY), dma(NZ),
        ],
        compiler_params=pltpu.CompilerParams(
            collective_id=0, has_side_effects=True, vmem_limit_bytes=48 << 20
        ),
        name="newton_schulz",
    )(momentum)


def solution(mesh):
    return jax.shard_map(
        local,
        mesh=mesh,
        in_specs=(P("rows", "cols"),),
        out_specs=P("rows", "cols"),
        check_vma=False,
    )
```

```python
import jax
import jax.numpy as jnp
from jax import lax
from jax.experimental import pallas as pl
from jax.experimental.pallas import tpu as pltpu
from jax.sharding import PartitionSpec as P

ROWS = 25600

coef_a = 3.4445
coef_b = -4.775
coef_c = 2.0315

NZ, NY, NX = 8, 4, 4
NB = 8
EARLY = 4
UP = 224
START = 7
MESH = pl.DeviceIdType.MESH
F32, BF16 = jnp.float32, jnp.bfloat16


def kernel(
    x_hbm, o_ref, xx, sb, rb, eb, yb, qb, zb, tot, gl, gr, pf, lt,
    loc, xs, cs, zs, zqs, ys, es, as_, gzs, gxs, gcs, pzs, pcs,
    wr, xr, xr2, vyr, cr, zr, zqr, yr, ar, gzr, gxr, gcr, pzr, pcr,
):
    m, w = x_hbm.shape
    h = w // 2
    q = qb.shape[1]
    hp = NY * q
    ql = h - (NY - 1) * q
    cut = -(-h // 32) * 16
    mid = -(-m // 32) * 16
    up = UP
    qtr = -(-up // 32) * 16
    r, c = lax.axis_index("rows"), lax.axis_index("cols")
    z, yh, k = r // (NY * 2), lax.rem(r // 2, NY), lax.rem(r, 2)
    yl, x = c // NX, lax.rem(c, NX)

    def rid(z=z, yh=yh, k=k):
        return (z * NY + yh) * 2 + k

    def cid(yl=yl, x=x):
        return yl * NX + x

    def at_x(d):
        return lax.rem(x + d, NX)

    def at_z(d):
        return lax.rem(z + d, NZ)

    def at_y(d):
        return lax.rem(yh + d, NY)

    core = (rid(k=1 - k), c)
    ypair = (r, cid(yl=1 - yl))
    xdev = [(r, cid(x=at_x(d))) for d in range(NX)]
    zdev = [(rid(z=at_z(d)), c) for d in range(NZ)]
    ydev = [(rid(yh=at_y(d)), c) for d in range(NY)]

    def copy(src, dst, ss, rs, to):
        return pltpu.make_async_remote_copy(
            src_ref=src, dst_ref=dst, send_sem=ss, recv_sem=rs, device_id=to, device_id_type=MESH
        )

    def send(src, dst, ss, rs, to):
        copy(src, dst, ss, rs, to).start()

    def arrived(dst, rs):
        copy(dst, dst, loc, rs, core).wait_recv()

    def sent(src, ss):
        copy(src, src, ss, loc, core).wait_send()

    mine = xx.at[c, pl.ds(k * m, m)]
    own = pltpu.make_async_copy(x_hbm, mine, loc)
    own.start()
    barrier = pltpu.get_barrier_semaphore()
    partners = [core, ypair] + xdev[1:] + [(r, cid(yl=1 - yl, x=at_x(d))) for d in (1, 2, 3)] + zdev[1:] + ydev[1:]
    for to in partners:
        pl.semaphore_signal(barrier, inc=1, device_id=to, device_id_type=MESH)
    pl.semaphore_wait(barrier, len(partners))
    own.wait()

    xslots = [cid(x=at_x(d)) for d in range(NX)]
    xslots2 = [cid(yl=1 - yl, x=at_x(d)) for d in range(NX)]
    zslots = [at_z(d) for d in range(NZ)]
    order = [xslots[0], xslots2[0]] + [xslots[d] for d in (1, 3, 2)] + [xslots2[d] for d in (1, 3, 2)]
    c2 = order[1]

    def owner(b):
        return lax.rem(b, NX) * 2 + b // NX

    def block(s):
        return s % 2 * NX + s // 2 if isinstance(s, int) else lax.rem(s, 2) * NX + s // 2

    def ring_hop(buf, ss, rs, dev, slots, hop, right, n):
        reach = len(slots) // 2 - (right == n % 2)
        if hop > reach:
            return
        s = slots[-hop if right else hop] if hop else slots[0]
        if hop:
            arrived(buf(s, n), rs(s, n))
        if hop < reach:
            send(buf(s, n), buf(s, n), ss, rs(s, n), dev[1 if right else -1])

    def ring_step(*args):
        for right, n in ((1, 0), (0, 1), (1, 1), (0, 0)):
            ring_hop(*args, right, n)

    def half(b):
        return xx.at[b, pl.ds(k * m, m)]

    def other(b):
        return xx.at[b, pl.ds((1 - k) * m, m)]

    def x_half(b, n):
        return xx.at[b, pl.ds(k * m + n * mid, m - mid if n else mid)]

    def x_quarter(b, n):
        return xx.at[b, pl.ds(k * m + n * qtr, up - qtr if n else qtr)]

    def x_rest(i):
        return xx.at[order[i], pl.ds(k * m + up, m - up)]

    def over(i):
        send(x_rest(i), x_rest(i), xs, vyr.at[lax.rem(order[i], NX)], ypair)

    def back(i):
        arrived(x_rest(i), vyr.at[lax.rem(order[i], NX)])

    def hand(i):
        send(half(order[i]), half(order[i]), cs, cr.at[order[i]], core)

    def quarter(p):
        return pl.ds(pl.multiple_of(p * q, q), q)

    def with_quarter(p, do):
        @pl.when(p < NY - 1)
        def _():
            do(quarter(p), q)

        @pl.when(p == NY - 1)
        def _():
            do(pl.ds((NY - 1) * q, ql), ql)

    def spread(src, dst, ss, rs):
        for d in (1, 3, 2):
            with_quarter(at_y(d), lambda rows, n: send(src.at[rows], dst.at[yh, pl.ds(0, n)], ss, rs, ydev[d]))

    def quarters_in(buf, rs):
        with_quarter(yh, lambda rows, n: arrived(buf.at[pl.ds(0, NY - 1), pl.ds(0, n)], rs))

    def to_owner(i, src, dst, ss, rs):
        to = owner(order[i])

        @pl.when(to != z)
        def _():
            send(src, dst.at[z], ss, rs, (rid(z=to), c))

        @pl.when(to == z)
        def _():
            dst[z] = src[...]

    def add_up(buf, out):
        value = buf[0].astype(F32)
        for s in range(1, buf.shape[0]):
            value = value + buf[s].astype(F32)
        out[...] = value.astype(out.dtype)

    def partial(i):
        b = order[i]
        if i:
            arrived(other(b), cr.at[b])
        sb[i] = jnp.dot(lt[...], xx[b], preferred_element_type=F32).astype(BF16)
        if i < EARLY:
            to_owner(i, sb.at[i], rb, zs, zr)
        else:
            j = i - EARLY
            yb[j, yh] = sb[i, quarter(yh)]
            spread(sb.at[i], yb.at[j], ys, yr.at[j])

    def late(i):
        j = i - EARLY
        quarters_in(yb.at[j], yr.at[j])
        add_up(yb.at[j], qb.at[j])
        to_owner(i, qb.at[j], zb, zqs, zqr)

    rring = (x_half, xs, lambda b, n: xr.at[lax.rem(b, NX), n], xdev, xslots)
    rring2 = (x_quarter, xs, lambda b, n: xr2.at[lax.rem(b, NX), n], xdev, xslots2)
    send(half(c), half(c), xs, wr, ypair)
    ring_step(*rring, 0)
    hand(0)
    pick = (
        lax.broadcasted_iota(jnp.int32, (hp, w), 1) == lax.broadcasted_iota(jnp.int32, (hp, w), 0) + k * h
    ).astype(BF16)
    arrived(other(c), cr.at[c])
    lt[...] = lax.dot_general(
        pick, xx[c], (((1,), (1,)), ((), ())), preferred_element_type=F32
    ).astype(BF16)
    partial(0)
    ring_step(*rring, 1)
    over(2)
    over(3)
    hand(2)
    hand(3)
    arrived(half(c2), wr)
    ring_step(*rring2, 0)
    hand(1)
    partial(2)
    partial(3)
    partial(1)
    ring_step(*rring, 2)
    over(4)
    hand(4)
    ring_step(*rring2, 1)
    for i in (5, 6):
        back(i)
        hand(i)
    partial(4)
    partial(5)
    partial(6)
    ring_step(*rring2, 2)
    back(7)
    hand(7)
    partial(7)
    mine_early = owner(order[0]) == z
    for i in range(1, EARLY):
        mine_early = jnp.logical_or(mine_early, owner(order[i]) == z)

    def start_early():
        @pl.when(mine_early)
        def _():
            arrived(rb.at[pl.ds(0, NZ - 1)], zr)
            add_up(rb, eb)
            yb[NB - EARLY, yh] = eb[quarter(yh)]
            spread(eb, yb.at[NB - EARLY], es, yr.at[NB - EARLY])

    for i in range(EARLY, NB):
        if i == START:
            start_early()
        late(i)
    if START == NB:
        start_early()

    @pl.when(mine_early)
    def _():
        quarters_in(yb.at[NB - EARLY], yr.at[NB - EARLY])
        add_up(yb.at[NB - EARLY], tot)

    @pl.when(jnp.logical_not(mine_early))
    def _():
        arrived(zb.at[pl.ds(0, NZ - 1)], zqr)
        add_up(zb, tot)

    top = pl.ds(k * h, h)
    low = pl.ds((1 - k) * h, h)
    columns = [ypair] + [xdev[d] for d in (1, 3, 2)] + [(r, xslots2[d]) for d in (1, 3, 2)]

    def over_z(s, rows, j, hop, right):
        if hop < NZ // 2 - (right == j % 2):
            g = gl.at[s, rows]
            send(g, g, gzs, gzr.at[s, j], zdev[1 if right else -1])

    def set_off(j):
        def go(rows, n):
            g = gl.at[z, rows]
            if j == 0:
                gl[z, rows] = (tot[pl.ds(0, n)] / ROWS).astype(BF16)
                for d in (1, 3, 2):
                    send(g, g, as_, ar.at[NY - d], ydev[d])
            else:
                arrived(g, ar.at[j])
            for right in (1, 0):
                over_z(z, rows, j, 0, right)
            for to in columns:
                send(g, gr.at[c, pl.ds(pl.multiple_of(k * h + rows.start, 16), n)], gxs, gxr.at[c], to)

        with_quarter(at_y(j), go)

    def hops(step, js):
        for j in js:
            for right in (1, 0):
                if step <= NZ // 2 - (right == j % 2):
                    s = zslots[-step if right else step]

                    def go(rows, n):
                        arrived(gl.at[s, rows], gzr.at[s, j])
                        over_z(s, rows, j, step, right)

                    with_quarter(at_y(j), go)

    def hand_on(slots):
        for b in slots:
            send(gr.at[b, top], gr.at[b, top], gcs, gcr, core)

    def columns_in(slots):
        for b in slots:
            arrived(gr.at[b, top], gxr.at[b])
            hand_on([b])

    set_off(0)
    set_off(1)
    set_off(3)
    hops(1, (0,))
    set_off(2)
    gram = gl[z]
    gr[c, top, :] = gram
    hand_on([c])
    hops(1, (1, 3))
    hops(2, (0,))
    hops(1, (2,))
    hops(2, (1, 3))
    hops(3, (0,))
    hops(2, (2,))
    columns_in(order[1:4])
    hops(3, (1, 3))
    hops(3, (2,))
    columns_in(order[4:])
    def square_term(s):
        return jnp.dot(gl[s], gr[block(s)], preferred_element_type=F32)

    arrived(gr.at[:, pl.ds(0, h)], gcr)
    square = square_term(z)
    for d in (1, 7, 2, 6, 3, 5):
        square = square + square_term(zslots[d])
    hops(4, (0, 1, 3, 2))
    square = square + square_term(zslots[4])
    pf[z, top, :] = (coef_b * gram.astype(F32) + coef_c * square).astype(BF16)
    def p_row(s, n):
        return pf.at[s, pl.ds(k * h + n * q, min(q, h - n * q))]

    def ring_step4(*args):
        for right, n in ((1, 0), (0, 1), (1, 2), (0, 3), (1, 1), (0, 0), (1, 3), (0, 2)):
            ring_hop(*args, right, n)

    pring = (p_row, pzs, lambda s, n: pzr.at[s, n], zdev, zslots)

    def hand_over(slots):
        for s in slots:
            send(pf.at[s, top], pf.at[s, top], pcs, pcr.at[s], core)

    def term(s):
        arrived(pf.at[s, low], pcr.at[s])
        return lax.dot_general(
            xx[block(s), pl.ds(k * m, m)], pf[s], (((1,), (1,)), ((), ())), preferred_element_type=F32
        )

    ring_step4(*pring, 0)
    hand_over([z])
    update = None
    held = [z]
    for step in range(1, 5):
        ring_step4(*pring, step)
        got = [zslots[-step], zslots[step]] if step < 4 else [zslots[4]]
        hand_over(got)
        for s in held:
            update = term(s) if update is None else update + term(s)
        held = got
    for s in held:
        update = update + term(s)
    o_ref[...] = (coef_a * xx[c, pl.ds(k * m, m)].astype(F32) + update).astype(BF16)

    sent(xx.at[pl.ds(0, NB - 1), pl.ds(0, m)], xs)
    sent(xx.at[:, pl.ds(0, m)], cs)

    @pl.when(mine_early)
    def _():
        sent(sb.at[pl.ds(0, EARLY - 1)], zs)
        sent(qb, zqs)
        with_quarter(yh, lambda rows, n: sent(eb.at[pl.ds(0, h - n)], es))

    @pl.when(jnp.logical_not(mine_early))
    def _():
        sent(sb.at[pl.ds(0, EARLY)], zs)
        sent(qb.at[pl.ds(0, NB - EARLY - 1)], zqs)

    with_quarter(yh, lambda rows, n: sent(sb.at[pl.ds(0, NB - EARLY), pl.ds(0, h - n)], ys))
    with_quarter(yh, lambda rows, n: sent(gl.at[pl.ds(0, NY - 1), pl.ds(0, n)], as_))
    sent(gl.at[pl.ds(0, NZ - 1)], gzs)
    sent(gr.at[pl.ds(0, NB - 1), pl.ds(0, h)], gxs)
    sent(gr.at[:, pl.ds(0, h)], gcs)
    sent(pf.at[pl.ds(0, NZ - 1), pl.ds(0, h)], pzs)
    sent(pf.at[:, pl.ds(0, h)], pcs)


def local(momentum):
    m, w = momentum.shape
    h = w // 2
    q = -(-h // (16 * NY)) * 16
    dma = lambda *n: pltpu.SemaphoreType.DMA(n)
    one = pltpu.SemaphoreType.DMA
    return pl.pallas_call(
        kernel,
        out_shape=jax.ShapeDtypeStruct((m, w), BF16),
        in_specs=[pl.BlockSpec(memory_space=pl.ANY)],
        out_specs=pl.BlockSpec(memory_space=pltpu.VMEM),
        scratch_shapes=[
            pltpu.VMEM((NB, 2 * m, w), BF16),
            pltpu.VMEM((NB, NY * q, w), BF16),
            pltpu.VMEM((NZ, NY * q, w), BF16),
            pltpu.VMEM((NY * q, w), BF16),
            pltpu.VMEM((NB - EARLY + 1, NY, q, w), BF16),
            pltpu.VMEM((NB - EARLY, q, w), BF16),
            pltpu.VMEM((NZ, q, w), BF16),
            pltpu.VMEM((q, w), F32),
            pltpu.VMEM((NZ, h, w), BF16),
            pltpu.VMEM((NB, w, w), BF16),
            pltpu.VMEM((NZ, w, w), BF16),
            pltpu.VMEM((NY * q, 2 * m), BF16),
            one, one, one, one, one, one, one, one, one, one, one, one, one,
            one, dma(NX, 2), dma(NX, 2), dma(NX), dma(NB), one, one, dma(NB - EARLY + 1), dma(NY),
            dma(NZ, NY), dma(NB), one, dma(NZ, NY), dma(NZ),
        ],
        compiler_params=pltpu.CompilerParams(
            collective_id=0, has_side_effects=True, vmem_limit_bytes=48 << 20
        ),
        name="newton_schulz",
    )(momentum)


def solution(mesh):
    return jax.shard_map(
        local,
        mesh=mesh,
        in_specs=(P("rows", "cols"),),
        out_specs=P("rows", "cols"),
        check_vma=False,
    )
```
